128 devices in a mesh: ctx: 32 (over y_hi, z, x), cand: 4 (over y_lo, core).
Axes of the slice: x: 4, y: 4 (y_hi: 2, y_lo: 2; y = y_hi * 2 + y_lo), z: 4, core: 2. Of those that a mesh axis runs over, the one named last changes fastest.
Arguments:
- history: bfloat16 [32768, 1024], P('ctx'), may hold values from -6 to 6
- candidates: bfloat16 [4096, 1024], P('ctx'), may hold values from -6 to 6
- history_valid: int32 [32768], P('ctx'), may hold values 0 or 1
- history_surface: int32 [32768], P('ctx'), may hold values from 0 to 7
- candidate_surface: int32 [4096], P('ctx'), may hold values from 0 to 7
- candidate_cutoff: int32 [4096], P('ctx'), may hold values from 1 to 32768
- gain_in: float32 [1024], replicated, may hold values from 0.1 to 1.9
- w_uvqk: bfloat16 [1024, 4, 1024], P(None, None, 'cand'), may hold values from -0.1875 to 0.1875
- gain_out: float32 [1024], P('cand'), may hold values from 0.1 to 1.9
- w_out: bfloat16 [1024, 1024], P('cand'), may hold values from -0.25 to 0.25
Outputs:
- history_out: bfloat16 [32768, 1024], P('ctx', 'cand')
- candidate_out: bfloat16 [4096, 1024], P('ctx', 'cand')
The draws below stay inside these ranges and needn't reach their ends.
All inputs are finite; a program needn't handle non-finite values. No bound on the sum of `history_valid` on one device may be relied on, other than what follows from the above.
Results may differ from the reference program's by a relative error of at most 0.0062.
Values may be sent and summed in bfloat16 or wider, within the bound.
A program may use at most 128 MiB of HBM per device.

```python
import math
import jax
import jax.numpy as jnp
from jax import lax

D = 1024
HEADS = 8
HEAD = 128
SURFACES = 8
H_DEV = 1024
HIST = 32768
CANDS = 4096
HD = 1024
WIN = 2048
N_CTX = 32


def set_ends(values, rng, least, high):
    index_at = [jax.random.randint(jax.random.fold_in(rng, axis), (), 0, length) for axis, length in enumerate(values.shape)]
    longest = values.shape.index(max(values.shape))
    next_to = index_at[:longest] + [(index_at[longest] + 1) % values.shape[longest]] + index_at[longest + 1:]
    return values.at[tuple(index_at)].set(least).at[tuple(next_to)].set(high)


def with_spikes(drawn, stream_key, source, target, shards_of, factor):
    owner, partner = [(jnp.arange(drawn.shape[dim]) // (drawn.shape[dim] // shards_of)).reshape([-1 if axis == dim else 1 for axis in range(drawn.ndim)]) for dim in (source, target)]
    chosen = jax.random.permutation(stream_key, shards_of)[partner]
    strong = (owner == chosen) | (owner == (partner + shards_of // 2) % shards_of)
    return jnp.where(strong, factor * drawn, drawn)


def levels(key, extent, shards, low, top_value):
    loudness = 1.0
    for axis_at, parts in shards:
        steps = jax.random.uniform(jax.random.fold_in(jax.random.fold_in(key, 6), axis_at), (parts,), jnp.float32, low / len(shards), top_value / len(shards))
        loudness = loudness * jnp.repeat(jnp.exp(steps), extent[axis_at] // parts).reshape((-1,) + (1,) * (len(extent) - 1 - axis_at))
    return loudness


def noise(rng, shape, deviation, most, split=(), held_as=jnp.bfloat16):
    drawn = jax.random.normal(rng, shape, jnp.float32) * deviation
    if len(split) > 0:
        drawn = levels(rng, shape, split, -0.22, 0.18) * drawn
    return jnp.clip(drawn, min=-most, max=most).astype(held_as)


def gaussian_with(stream_key, extent, width, bound, cuts, heavy, kind=jnp.bfloat16):
    drawn = width * jax.random.normal(stream_key, extent, jnp.float32)
    if cuts:
        drawn = drawn * levels(stream_key, extent, cuts, -0.22, 0.18)
    return jnp.clip(with_spikes(drawn, jax.random.fold_in(stream_key, 3), *heavy), -bound, bound).astype(kind)


def setup_inputs(seed: int = 0) -> dict:
    arg_keys = jax.random.split(jax.random.key(seed), 11)
    return {
        "history": noise(arg_keys[0], (HIST, D), 1.0, 6.0, ((0, 32),)),
        "candidates": noise(arg_keys[1], (CANDS, D), 1.0, 6.0, ((0, 32),)),
        "history_valid": set_ends((jax.random.randint(arg_keys[2], (HIST,), 0, 8) < 7).astype(jnp.int32), jax.random.fold_in(arg_keys[2], 1), 0, 1),
        "history_surface": set_ends(jax.random.randint(arg_keys[3], (HIST,), 0, SURFACES), jax.random.fold_in(arg_keys[3], 1), 0, SURFACES - 1).astype(jnp.int32),
        "candidate_surface": set_ends(jax.random.randint(arg_keys[4], (CANDS,), 0, SURFACES), jax.random.fold_in(arg_keys[4], 1), 0, SURFACES - 1).astype(jnp.int32),
        "candidate_cutoff": set_ends(jax.random.randint(arg_keys[5], (CANDS,), 1, HIST + 1), jax.random.fold_in(arg_keys[5], 1), 1, HIST).astype(jnp.int32),
        "gain_in": jnp.clip(1.0 + 0.18 * jax.random.normal(arg_keys[6], (D,), jnp.float32), 0.1, 1.9),
        "w_uvqk": noise(arg_keys[7], (D, 4, HD), D ** -0.5, 0.1875, ((2, 4),)),
        "gain_out": jnp.clip(1.0 + 0.18 * jax.random.normal(arg_keys[8], (HD,), jnp.float32), 0.1, 1.9),
        "w_out": gaussian_with(arg_keys[9], (HD, D), HD ** -0.5, 0.25, ((0, 4),), (0, 1, 4, 2.0)),
    }


EPS = 1e-05

def layer_in(inputs, gain):
    values_f = inputs.astype(jnp.float32)
    center = values_f - lax.optimization_barrier(jnp.mean(values_f, axis=-1, keepdims=True))
    spread = lax.optimization_barrier(jnp.mean(center * center, axis=-1, keepdims=True))
    return (center * lax.rsqrt(spread + EPS) * gain).astype(jnp.bfloat16)

def project(inputs, gain_in, w_uvqk):
    normed = layer_in(inputs, gain_in)
    flat = w_uvqk.reshape(w_uvqk.shape[0], 4 * HD)
    proj = jax.nn.silu(jnp.dot(normed, flat, preferred_element_type=jnp.float32)).astype(jnp.bfloat16)
    return proj.reshape(inputs.shape[0], 4, HEADS, HEAD)

def reference(history, candidates, history_valid, history_surface, candidate_surface, candidate_cutoff, gain_in, w_uvqk, gain_out, w_out):
    scale = 1.0 / math.sqrt(HEAD)
    hist_proj = project(history, gain_in, w_uvqk)
    cand_proj = project(candidates, gain_in, w_uvqk)
    hist_keys = jnp.concatenate([jnp.zeros((WIN, HEADS, HEAD), jnp.bfloat16), hist_proj[:, 3]], 0)
    hist_vals = jnp.concatenate([jnp.zeros((WIN, HEADS, HEAD), jnp.bfloat16), hist_proj[:, 1]], 0)
    valid_pad = jnp.concatenate([jnp.zeros((WIN,), jnp.int32), history_valid], 0)
    row_idx = jnp.arange(H_DEV, dtype=jnp.int32)
    col_idx = jnp.arange(3 * H_DEV, dtype=jnp.int32)

    def hist_block(block):
        start = (block * H_DEV).astype(jnp.int32)
        queries = lax.dynamic_slice_in_dim(hist_proj[:, 2], start, H_DEV, 0).astype(jnp.float32)
        key_rows = lax.dynamic_slice_in_dim(hist_keys, start, 3 * H_DEV, 0).astype(jnp.float32)
        val_rows = lax.dynamic_slice_in_dim(hist_vals, start, 3 * H_DEV, 0).astype(jnp.float32)
        okay = lax.dynamic_slice_in_dim(valid_pad, start, 3 * H_DEV, 0)
        mask = (col_idx[None, :] > row_idx[:, None]) & (col_idx[None, :] <= row_idx[:, None] + WIN) & (okay[None, :] == 1)
        scores = jnp.einsum('qhd,khd->hqk', queries, key_rows) * scale
        weights = jnp.where(mask[None], jax.nn.silu(scores), 0.0).astype(jnp.bfloat16)
        return jnp.einsum('hqk,khd->qhd', weights.astype(jnp.float32), val_rows)
    hist_attn = lax.map(hist_block, jnp.arange(N_CTX, dtype=jnp.int32)).reshape(HIST, HD)
    cand_q = cand_proj[:, 2].astype(jnp.float32)

    def cand_step(total, block):
        start = (block * H_DEV).astype(jnp.int32)
        key_rows = lax.dynamic_slice_in_dim(hist_proj[:, 3], start, H_DEV, 0).astype(jnp.float32)
        val_rows = lax.dynamic_slice_in_dim(hist_proj[:, 1], start, H_DEV, 0).astype(jnp.float32)
        okay = lax.dynamic_slice_in_dim(history_valid, start, H_DEV, 0)
        surface = lax.dynamic_slice_in_dim(history_surface, start, H_DEV, 0)
        position = start + jnp.arange(H_DEV, dtype=jnp.int32)
        mask = (okay[None, :] == 1) & (position[None, :] < candidate_cutoff[:, None]) & (surface[None, :] == candidate_surface[:, None])
        scores = jnp.einsum('qhd,khd->hqk', cand_q, key_rows) * scale
        weights = jnp.where(mask[None], jax.nn.silu(scores), 0.0).astype(jnp.bfloat16)
        return (total + jnp.einsum('hqk,khd->qhd', weights.astype(jnp.float32), val_rows), None)
    cand_attn, _ = lax.scan(cand_step, jnp.zeros((CANDS, HEADS, HEAD), jnp.float32), jnp.arange(N_CTX, dtype=jnp.int32))
    self_score = lax.optimization_barrier(jnp.sum(cand_q * cand_proj[:, 3].astype(jnp.float32), axis=-1)) * scale
    self_weight = jax.nn.silu(self_score).astype(jnp.bfloat16).astype(jnp.float32)
    cand_attn = (cand_attn + self_weight[..., None] * cand_proj[:, 1].astype(jnp.float32)).reshape(CANDS, HD)

    def finish(inputs, attn, proj):
        mean_row = lax.optimization_barrier(jnp.mean(attn, axis=-1, keepdims=True))
        square_row = lax.optimization_barrier(jnp.mean(attn * attn, axis=-1, keepdims=True))
        update = proj[:, 0].reshape(attn.shape[0], HD).astype(jnp.float32)
        gated = ((attn - mean_row) * lax.rsqrt(square_row - mean_row * mean_row + EPS) * gain_out * update).astype(jnp.bfloat16)
        mixed = jnp.dot(gated, w_out, preferred_element_type=jnp.float32)
        return (inputs.astype(jnp.float32) + mixed).astype(jnp.bfloat16)
    return (finish(history, hist_attn, hist_proj), finish(candidates, cand_attn, cand_proj))
```

```python
import math

import jax
import jax.numpy as jnp
from jax import lax
from jax.sharding import PartitionSpec as P

HEAD = 128


EPS = 1e-05


def from_behind(block, axis, distance):
    devices = range(lax.axis_size(axis))
    route = [(i - distance, i) for i in devices if i - distance in devices]
    return lax.ppermute(block, axis, route)


def layer_in(inputs, gain):
    values_f = inputs.astype(jnp.float32)
    center = values_f - jnp.mean(values_f, axis=-1, keepdims=True)
    spread = jnp.mean(center * center, axis=-1, keepdims=True)
    return (center * lax.rsqrt(spread + EPS) * gain).astype(jnp.bfloat16)


def split_heads(matrix):
    return matrix.reshape(matrix.shape[0], matrix.shape[1] // HEAD, HEAD)


def cand_block(queries, cutoff, surface, key_rows, val_rows, key_surface, position):
    scale = 1.0 / math.sqrt(HEAD)
    mask = (
        (position[None, :] < cutoff[:, None])
        & (key_surface[None, :] == surface[:, None])
    )
    scores = (
        jnp.einsum(
            "qhd,khd->hqk",
            split_heads(queries),
            split_heads(key_rows),
            preferred_element_type=jnp.float32,
        )
        * scale
    )
    weights = jnp.where(mask[None], jax.nn.silu(scores), 0.0).astype(jnp.bfloat16)
    summed = jnp.einsum(
        "hqk,khd->qhd", weights, split_heads(val_rows), preferred_element_type=jnp.float32
    )
    return summed.reshape(queries.shape[0], queries.shape[1])


def shards(
    history,
    candidates,
    history_valid,
    history_surface,
    candidate_surface,
    candidate_cutoff,
    gain_in,
    w_uvqk,
    gain_out,
    w_out,
):
    hist_rows = history.shape[0]
    cand_rows = candidates.shape[0]
    local_width = w_uvqk.shape[2]
    scale = 1.0 / math.sqrt(HEAD)
    inputs = jnp.concatenate([history, candidates], 0)
    normed = layer_in(inputs, gain_in)
    flat = w_uvqk.reshape(w_uvqk.shape[0], 4 * local_width)
    proj = jax.nn.silu(jnp.dot(normed, flat, preferred_element_type=jnp.float32)).astype(
        jnp.bfloat16
    )
    proj = proj.reshape(inputs.shape[0], 4, local_width)
    update = proj[:, 0]
    hist_vals = proj[:hist_rows, 1]
    hist_query = proj[:hist_rows, 2]
    hist_keys = proj[:hist_rows, 3]
    cand_vals = proj[hist_rows:, 1]
    cand_query = proj[hist_rows:, 2]
    cand_keys = proj[hist_rows:, 3]
    hist_vals = jnp.where(history_valid[:, None] == 1, hist_vals, 0).astype(jnp.bfloat16)
    both = jnp.concatenate([hist_keys, hist_vals], 1)
    first_back = from_behind(both, "ctx", 1)
    second_back = from_behind(both, "ctx", 2)
    window_keys = jnp.concatenate(
        [second_back[:, :local_width], first_back[:, :local_width], hist_keys], 0
    )
    window_vals = jnp.concatenate(
        [second_back[:, local_width:], first_back[:, local_width:], hist_vals], 0
    )
    limits = jnp.concatenate(
        [candidate_cutoff // 256, candidate_cutoff % 256, candidate_surface, candidate_surface]
    )
    limits = jnp.zeros((16, local_width), jnp.bfloat16).at[:2].set(
        limits.reshape(2, local_width).astype(jnp.bfloat16)
    )
    asked = lax.all_gather(jnp.concatenate([cand_query, limits], 0), "ctx", axis=0)
    row_idx = jnp.arange(hist_rows, dtype=jnp.int32)
    col_idx = jnp.arange(3 * hist_rows, dtype=jnp.int32)
    window_mask = (
        (col_idx[None, :] > row_idx[:, None])
        & (col_idx[None, :] <= row_idx[:, None] + 2 * hist_rows)
    )
    scores = (
        jnp.einsum(
            "qhd,khd->hqk",
            split_heads(hist_query),
            split_heads(window_keys),
            preferred_element_type=jnp.float32,
        )
        * scale
    )
    weights = jnp.where(window_mask[None], jax.nn.silu(scores), 0.0).astype(jnp.bfloat16)
    hist_attn = jnp.einsum(
        "hqk,khd->qhd", weights, split_heads(window_vals), preferred_element_type=jnp.float32
    )
    hist_attn = hist_attn.reshape(hist_rows, local_width)
    every_query = asked[:, :cand_rows].reshape(-1, local_width)
    told = asked[:, cand_rows : cand_rows + 2].astype(jnp.int32)
    every_cutoff = (told[:, 0, :cand_rows] * 256 + told[:, 0, cand_rows:]).reshape(-1)
    every_surface = told[:, 1, :cand_rows].reshape(-1)
    position = lax.axis_index("ctx") * hist_rows + jnp.arange(hist_rows, dtype=jnp.int32)
    partial = cand_block(
        every_query,
        every_cutoff,
        every_surface,
        hist_keys,
        hist_vals,
        history_surface,
        position,
    )
    cand_attn = lax.psum_scatter(partial, "ctx", scatter_dimension=0, tiled=True)
    self_score = (
        jnp.sum(
            split_heads(cand_query).astype(jnp.float32)
            * split_heads(cand_keys).astype(jnp.float32),
            axis=-1,
        )
        * scale
    )
    self_weight = jax.nn.silu(self_score).astype(jnp.bfloat16).astype(jnp.float32)
    self_term = self_weight[..., None] * split_heads(cand_vals).astype(jnp.float32)
    cand_attn = cand_attn + self_term.reshape(cand_rows, local_width)
    attn = jnp.concatenate([hist_attn, cand_attn], 0)
    row_sums, row_squares = lax.psum(
        (jnp.sum(attn, axis=-1), jnp.sum(attn * attn, axis=-1)), "cand"
    )
    full_width = local_width * lax.axis_size("cand")
    mean_row = (row_sums / full_width)[:, None]
    square_row = (row_squares / full_width)[:, None]
    gated = (
        (attn - mean_row)
        * lax.rsqrt(square_row - mean_row * mean_row + EPS)
        * gain_out
        * update.astype(jnp.float32)
    ).astype(jnp.bfloat16)
    mixed = jnp.dot(gated, w_out, preferred_element_type=jnp.float32)
    shares = lax.psum_scatter(mixed, "cand", scatter_dimension=1, tiled=True)
    out_cols = shares.shape[1]
    residual = lax.dynamic_slice_in_dim(inputs, lax.axis_index("cand") * out_cols, out_cols, 1)
    result = (residual.astype(jnp.float32) + shares).astype(jnp.bfloat16)
    return (result[:hist_rows], result[hist_rows:])


def solution(mesh):
    placed = (
        P("ctx", None),
        P("ctx", None),
        P("ctx"),
        P("ctx"),
        P("ctx"),
        P("ctx"),
        P(),
        P(None, None, "cand"),
        P("cand"),
        P("cand", None),
    )
    return jax.shard_map(
        shards,
        mesh=mesh,
        in_specs=placed,
        out_specs=(P("ctx", "cand"), P("ctx", "cand")),
        check_vma=False,
    )
```

```python
import functools
import math

import jax
import jax.numpy as jnp
from jax import lax
from jax.experimental import pallas as pl
from jax.experimental.pallas import tpu as pltpu
from jax.sharding import PartitionSpec as P

HEAD = 128
EPS = 1e-05
HALF_SCALE = 0.5 / math.sqrt(HEAD)
FAR = 2.0**60
CHUNK = 256
CARDS = 128
META = 16
BF16 = jnp.bfloat16
F32 = jnp.float32
MESH = pl.DeviceIdType.MESH
NT = (((1,), (1,)), ((), ()))

S_W, S_QY, S_QX, S_QZ = 0, 3, 4, 7
S_H1, S_H2 = 10, 14
S_PZ, S_PX, S_PY = 18, 21, 24
S_ST, S_G = 25, 40
N_SEM = 55


def silu_of_half(half):
    return half * jnp.tanh(half) + half


def kernel(
    x_ref, cx_ref, valid_ref, hsurf_ref, csurf_ref, ccut_ref, gin_ref, w_ref, gout_ref, wo_ref,
    oh_ref, oc_ref,
    kv, hkv, qh, uh, cp, kf, vt, qall, qf, lcb, own, pz, rz, px, rx, py, ry, attn, cattn, st, gf, wc,
    ssem, rsem,
):
    c = lax.axis_index("ctx")
    h = lax.axis_index("cand")
    yh, z, xx = c // 16, (c // 4) % 4, c % 4

    def at_x(d):
        return (yh * 16 + z * 4 + (xx + d + 4) % 4, h)

    def at_z(d):
        return (yh * 16 + ((z + d + 4) % 4) * 4 + xx, h)

    def at_y():
        return ((c + 16) % 32, h)

    def at_c(d):
        return ((c + d + 32) % 32, h)

    def at_h(d):
        return (c, (h + d) % 4)

    core_peer = (c, h + 1 - 2 * (h % 2))
    y_peer = (c, (h + 2) % 4)

    barrier = pltpu.get_barrier_semaphore()
    greeted = [at_h(1), at_h(2), at_h(3), at_y(), at_x(1), at_x(2), at_x(3), at_z(1), at_z(2), at_z(3)]
    greeted += [at_c(1), at_c(2), at_c(-1), at_c(-2)]
    for device in greeted:
        pl.semaphore_signal(barrier, inc=1, device_id=device, device_id_type=MESH)

    def remote(src, dst, slot, device):
        return pltpu.make_async_remote_copy(
            src_ref=src, dst_ref=dst, send_sem=ssem.at[slot], recv_sem=rsem.at[slot],
            device_id=device, device_id_type=MESH,
        )

    sent = []

    def send(*args):
        copy = remote(*args)
        copy.start()
        sent.append(copy)
        return copy

    def project(rows):
        values = rows.astype(F32)
        center = values - jnp.mean(values, axis=-1, keepdims=True)
        spread = jnp.mean(center * center, axis=-1, keepdims=True)
        normed = (center * lax.rsqrt(spread + EPS) * gin_ref[...]).astype(BF16)
        half = jnp.dot(normed, w_ref[...], preferred_element_type=F32) * 0.5
        return silu_of_half(half).astype(BF16)

    cp[...] = project(cx_ref[...])
    qall[0, 0, 0, 0:CARDS, :] = cp[:, 512:768]
    cut = ccut_ref[...]
    limits = jnp.concatenate([lax.shift_right_logical(cut, 8), cut & 255], 1).astype(F32)
    surf = csurf_ref[...].astype(F32)
    surf = jnp.concatenate([surf, surf], 1)
    row = lax.broadcasted_iota(jnp.int32, (META, 256), 0)
    qall[0, 0, 0, CARDS:, :] = jnp.where(row == 0, limits, jnp.where(row == 1, surf, 0.0)).astype(BF16)

    pl.semaphore_wait(barrier, len(greeted))
    q_y = send(qall.at[0, 0, 0], qall.at[0, 0, 1], S_QY, at_y())

    vt[...] = jnp.transpose(valid_ref[...].astype(F32))
    surf_t = jnp.transpose(hsurf_ref[...].astype(F32))
    lane = lax.broadcasted_iota(jnp.int32, (CARDS, 128), 1).astype(F32)
    for i in range(8):
        kf[i * 128 : i * 128 + 128, :] = jnp.where(surf_t[:, i : i + 1] == lane, 1.0, 0.0).astype(BF16)

    def hist_chunk(i):
        at = slice(i * CHUNK, i * CHUNK + CHUNK)
        proj = project(x_ref[at, :])
        okay = jnp.concatenate([vt[:, 2 * i : 2 * i + 1], vt[:, 2 * i + 1 : 2 * i + 2]], 0)
        uh[at, :] = proj[:, 0:256]
        qh[at, :] = proj[:, 512:768]
        kv[at, 0:256] = proj[:, 768:1024]
        kv[at, 256:512] = (proj[:, 256:512].astype(F32) * okay).astype(BF16)
        return send(kv.at[at], hkv.at[0, at], S_H1 + i, at_c(1))

    first = [hist_chunk(0)]
    q_y.wait_recv()
    q_x = [None] + [send(qall.at[0, 0], qall.at[0, d], S_QX + d - 1, at_x(d)) for d in (1, 2, 3)]
    first.append(hist_chunk(1))
    first.append(hist_chunk(2))
    for d in (1, 2, 3):
        q_x[d].wait_recv()
    q_z = [None] + [send(qall.at[0], qall.at[d], S_QZ + d - 1, at_z(d)) for d in (1, 2, 3)]
    first.append(hist_chunk(3))
    second = [None] * 4
    for i in (3, 2, 1, 0):
        at = slice(i * CHUNK, i * CHUNK + CHUNK)
        second[i] = send(kv.at[at], hkv.at[1, at], S_H2 + i, at_c(2))
    mine = pl.ds(pl.multiple_of(h * 256, 256), 256)
    into = []
    for d in (1, 2, 3):
        theirs = pl.ds(pl.multiple_of(((h + d) % 4) * 256, 256), 256)
        into.append(send(wo_ref.at[:, theirs], wc.at[mine, :], S_W + d - 1, at_h(d)))
    wc[mine, :] = wo_ref[:, mine]

    def attend(queries, keys, values, mask):
        half = lax.dot_general(queries, keys, NT, preferred_element_type=F32) * HALF_SCALE
        weights = silu_of_half(half)
        if mask is not None:
            weights = jnp.where(mask(weights.shape), weights, 0.0)
        return jnp.dot(weights.astype(BF16), values, preferred_element_type=F32)

    def hist_tile(keys_ref, j, lo, hi, mask):
        ks = slice(j * CHUNK, j * CHUNK + CHUNK)
        out = []
        for head in range(2):
            a, b = head * 128, head * 128 + 128
            out.append(attend(qh[lo:hi, a:b], keys_ref[ks, a:b], keys_ref[ks, 256 + a : 256 + b], mask))
        return jnp.concatenate(out, 1)

    def not_later(shape):
        return lax.broadcasted_iota(jnp.int32, shape, 1) <= lax.broadcasted_iota(jnp.int32, shape, 0)

    attn[...] = hist_tile(kv, 0, 0, 1024, not_later)
    for j in (1, 2, 3):
        attn[j * CHUNK :, :] += hist_tile(kv, j, j * CHUNK, 1024, not_later)

    start = (c * 1024).astype(F32)

    def cand_plane(dz):
        for dx in range(4):
            for dy in range(2):
                told = qall[dz, dx, dy, CARDS:, :].astype(F32)
                local = told[0:8, 0:128] * 256.0 + told[0:8, 128:256] - start
                both = jnp.where(
                    lax.broadcasted_iota(jnp.int32, (8, 128), 0) == 0, local, told[0:8, 0:128]
                )
                both = jnp.transpose(both)
                r = (dx * 2 + dy) * 128
                lcb[r : r + 128, :] = jnp.broadcast_to(both[:, 0:1], (128, 128))
                qf[r : r + 128, :] = jnp.where(both[:, 1:2] == lane, 0.0, -FAR).astype(BF16)

        heads = []
        for head in range(2):
            a, b = head * 128, head * 128 + 128
            queries = jnp.concatenate(
                [qall[dz, dx, dy, 0:CARDS, a:b] for dx in range(4) for dy in range(2)], 0
            )
            queries = jnp.concatenate([queries, qf[...]], 1)
            total = None
            for j in range(4):
                ks = slice(j * CHUNK, j * CHUNK + CHUNK)
                keys = jnp.concatenate([kv[ks, a:b], kf[ks, :]], 1)

                def mask(shape):
                    place = (lax.broadcasted_iota(jnp.int32, shape, 1) + j * CHUNK).astype(F32)
                    return place < jnp.concatenate([lcb[...], lcb[...]], 1)

                part = attend(queries, keys, kv[ks, 256 + a : 256 + b], mask)
                total = part if total is None else total + part
            heads.append(total)
        return jnp.concatenate(heads, 1)

    own[...] = cand_plane(0)
    p_z = [None] * 4
    for d in (1, 3, 2):
        q_z[d].wait_recv()
        pz[d - 1] = cand_plane(d).astype(BF16)
        p_z[d] = send(pz.at[d - 1], rz.at[d - 1], S_PZ + d - 1, at_z(-d))

    for i in range(4):
        first[i].wait_recv()

    @pl.when(c >= 1)
    def _():
        for j in range(4):
            attn[...] += hist_tile(hkv.at[0], j, 0, 1024, None)

    for d in (1, 3, 2):
        p_z[d].wait_recv()
    total = own[...]
    for d in (1, 2, 3):
        total += rz[d - 1].astype(F32)
    px[...] = total.astype(BF16)
    p_x = [None] + [
        send(px.at[pl.ds(d * 256, 256)], rx.at[d - 1], S_PX + d - 1, at_x(-d)) for d in (1, 2, 3)
    ]
    own[0:256, :] = total[0:256]

    full = 1024.0

    def chunk_rows(i):
        return (slice(i * CHUNK, i * CHUNK + CHUNK), CHUNK) if i < 4 else (slice(1024, 1152), CARDS)

    def stats_out(i, values):
        size = values.shape[0]
        sums = jnp.sum(values, axis=-1, keepdims=True)
        squares = jnp.sum(values * values, axis=-1, keepdims=True)
        spread = lax.broadcasted_iota(jnp.int32, (size, 128), 1)
        st[0, i, :, 0:size] = jnp.transpose(jnp.where(spread == 0, sums, squares))[0:8, :]
        return [
            send(st.at[0, i], st.at[d, i], S_ST + 3 * i + d - 1, at_h(d)) for d in (1, 2, 3)
        ]

    def gate_out(i, values, update, got):
        at, size = chunk_rows(i)
        for copy in got:
            copy.wait_recv()
        both = (st[0, i] + st[1, i] + st[2, i] + st[3, i])[:, 0:size] / full
        both = jnp.transpose(both)
        mean, square = both[:, 0:1], both[:, 1:2]
        gated = (values - mean) * lax.rsqrt(square - mean * mean + EPS) * gout_ref[...] * update.astype(F32)
        gf[at, mine] = gated.astype(BF16)
        block = gf.at[at, mine]
        return [
            send(block, block, S_G + 3 * i, core_peer),
            send(block, block, S_G + 3 * i + 1, y_peer),
        ]

    across = pl.ds(pl.multiple_of(((h + 2) % 4) * 256, 256), 256)

    def gate_forward(i, moving):
        at, _ = chunk_rows(i)
        moving[1].wait_recv()
        block = gf.at[at, across]
        moving.append(send(block, block, S_G + 3 * i + 2, core_peer))

    def finish(i, moving, rows_ref, out_ref):
        at, size = chunk_rows(i)
        moving[0].wait_recv()
        moving[2].wait_recv()
        where = at if i < 4 else slice(0, CARDS)
        mixed = jnp.dot(gf[at, :], wc[...], preferred_element_type=F32)
        out_ref[where, :] = (rows_ref[where, mine].astype(F32) + mixed).astype(BF16)

    got, moving = {}, {}
    for copy in into:
        copy.wait_recv()
    for i in (3, 2, 1, 0):
        second[i].wait_recv()

        @pl.when(c >= 2)
        def _():
            def later(shape):
                return (
                    lax.broadcasted_iota(jnp.int32, shape, 1) + i * CHUNK
                    > lax.broadcasted_iota(jnp.int32, shape, 0)
                )

            hi = i * CHUNK + CHUNK
            attn[0:hi, :] += hist_tile(hkv.at[1], i, 0, hi, later)

        at, _size = chunk_rows(i)
        got[i] = stats_out(i, attn[at, :])
        if i == 3:
            for d in (1, 2, 3):
                p_x[d].wait_recv()
            total = own[0:256, :]
            for d in (1, 2, 3):
                total += rx[d - 1].astype(F32)
            own[0:CARDS, :] = total[0:CARDS]
            py[...] = total[CARDS:]
            p_y = send(py, ry, S_PY, at_y())
        if i == 2:
            p_y.wait_recv()
            total = own[0:CARDS, :] + ry[...]
            selfs = []
            for head in range(2):
                a, b = head * 128, head * 128 + 128
                query = cp[:, 512 + a : 512 + b].astype(F32)
                key = cp[:, 768 + a : 768 + b].astype(F32)
                half = jnp.sum(query * key, axis=-1, keepdims=True) * HALF_SCALE
                weight = silu_of_half(half).astype(BF16).astype(F32)
                selfs.append(weight * cp[:, 256 + a : 256 + b].astype(F32))
            cattn[...] = total + jnp.concatenate(selfs, 1)
            got[4] = stats_out(4, cattn[...])
        if i <= 2:
            k = i + 1
            where = chunk_rows(k)[0]
            moving[k] = gate_out(k, attn[where, :], uh[where, :], got[k])
        if i == 1:
            moving[4] = gate_out(4, cattn[...], cp[:, 0:256], got[4])
            gate_forward(3, moving[3])
        if i == 0:
            gate_forward(2, moving[2])
            gate_forward(4, moving[4])
    moving[0] = gate_out(0, attn[0:CHUNK, :], uh[0:CHUNK, :], got[0])
    finish(3, moving[3], x_ref, oh_ref)
    gate_forward(1, moving[1])
    finish(2, moving[2], x_ref, oh_ref)
    finish(4, moving[4], cx_ref, oc_ref)
    gate_forward(0, moving[0])
    finish(1, moving[1], x_ref, oh_ref)
    finish(0, moving[0], x_ref, oh_ref)
    for copy in sent:
        copy.wait_send()


def shards(
    history,
    candidates,
    history_valid,
    history_surface,
    candidate_surface,
    candidate_cutoff,
    gain_in,
    w_uvqk,
    gain_out,
    w_out,
):
    vmem = pl.BlockSpec(memory_space=pltpu.VMEM)
    return pl.pallas_call(
        kernel,
        out_shape=(
            jax.ShapeDtypeStruct((1024, 256), BF16),
            jax.ShapeDtypeStruct((CARDS, 256), BF16),
        ),
        in_specs=[vmem] * 10,
        out_specs=(vmem, vmem),
        scratch_shapes=[
            pltpu.VMEM((1024, 512), BF16),
            pltpu.VMEM((2, 1024, 512), BF16),
            pltpu.VMEM((1024, 256), BF16),
            pltpu.VMEM((1024, 256), BF16),
            pltpu.VMEM((CARDS, 1024), BF16),
            pltpu.VMEM((1024, 128), BF16),
            pltpu.VMEM((128, 8), F32),
            pltpu.VMEM((4, 4, 2, CARDS + META, 256), BF16),
            pltpu.VMEM((1024, 128), BF16),
            pltpu.VMEM((1024, 128), F32),
            pltpu.VMEM((1024, 256), F32),
            pltpu.VMEM((3, 1024, 256), BF16),
            pltpu.VMEM((3, 1024, 256), BF16),
            pltpu.VMEM((1024, 256), BF16),
            pltpu.VMEM((3, 256, 256), BF16),
            pltpu.VMEM((CARDS, 256), F32),
            pltpu.VMEM((CARDS, 256), F32),
            pltpu.VMEM((1024, 256), F32),
            pltpu.VMEM((CARDS, 256), F32),
            pltpu.VMEM((4, 5, 8, 256), F32),
            pltpu.VMEM((1152, 1024), BF16),
            pltpu.VMEM((1024, 256), BF16),
            pltpu.SemaphoreType.DMA((N_SEM,)),
            pltpu.SemaphoreType.DMA((N_SEM,)),
        ],
        compiler_params=pltpu.CompilerParams(
            collective_id=0, has_side_effects=True, vmem_limit_bytes=56 * 2**20
        ),
        name="hstu",
    )(
        history,
        candidates,
        history_valid.reshape(8, 128),
        history_surface.reshape(8, 128),
        candidate_surface.reshape(1, CARDS),
        candidate_cutoff.reshape(1, CARDS),
        gain_in.reshape(1, 1024),
        w_uvqk.reshape(1024, 1024),
        gain_out.reshape(1, 256),
        w_out,
    )


def solution(mesh):
    placed = (
        P("ctx", None),
        P("ctx", None),
        P("ctx"),
        P("ctx"),
        P("ctx"),
        P("ctx"),
        P(),
        P(None, None, "cand"),
        P("cand"),
        P("cand", None),
    )
    return jax.shard_map(
        shards,
        mesh=mesh,
        in_specs=placed,
        out_specs=(P("ctx", "cand"), P("ctx", "cand")),
        check_vma=False,
    )
```

```python
import functools
import math

import jax
import jax.numpy as jnp
from jax import lax
from jax.experimental import pallas as pl
from jax.experimental.pallas import tpu as pltpu
from jax.sharding import PartitionSpec as P

HEAD = 128
EPS = 1e-05
HALF_SCALE = 0.5 / math.sqrt(HEAD)
FAR = 2.0**60
CHUNK = 256
CARDS = 128
META = 16
BF16 = jnp.bfloat16
F32 = jnp.float32
MESH = pl.DeviceIdType.MESH
NT = (((1,), (1,)), ((), ()))

N_SEM = 96


def silu_of_half(half):
    return half * jnp.tanh(half) + half


def kernel(
    x_ref, cx_ref, valid_ref, hsurf_ref, csurf_ref, ccut_ref, gin_ref, w_ref, gout_ref, wo_ref,
    oh_ref, oc_ref,
    nq, hx, hv, kv, hkv, qh, uh, cp, kf, qall, qf, lcb, own, pz, rz, px, rx, py, ry, attn, cattn, st, gf, wc,
    ssem, rsem,
):
    c = lax.axis_index("ctx")
    h = lax.axis_index("cand")
    yh, z, xx = c // 16, (c // 4) % 4, c % 4

    def at_x(d):
        return (yh * 16 + z * 4 + (xx + d + 4) % 4, h)

    def at_z(d):
        return (yh * 16 + ((z + d + 4) % 4) * 4 + xx, h)

    def at_y():
        return ((c + 16) % 32, h)

    def at_c(d):
        return ((c + d + 32) % 32, h)

    def at_h(d):
        return (c, (h + d) % 4)

    core_peer = (c, h + 1 - 2 * (h % 2))
    y_peer = (c, (h + 2) % 4)

    barrier = pltpu.get_barrier_semaphore()
    greeted = [at_h(1), at_h(2), at_h(3), at_y(), at_x(1), at_x(2), at_x(3), at_z(1), at_z(2), at_z(3)]
    greeted += [at_c(1), at_c(2), at_c(-1), at_c(-2)]
    for device in greeted:
        pl.semaphore_signal(barrier, inc=1, device_id=device, device_id_type=MESH)

    sent = []

    def send(src, dst, device):
        slot = len(sent)
        copy = pltpu.make_async_remote_copy(
            src_ref=src, dst_ref=dst, send_sem=ssem.at[slot], recv_sem=rsem.at[slot],
            device_id=device, device_id_type=MESH,
        )
        copy.start()
        sent.append(copy)
        return copy

    def normalize(rows):
        values = rows.astype(F32)
        center = values - jnp.mean(values, axis=-1, keepdims=True)
        spread = jnp.mean(center * center, axis=-1, keepdims=True)
        return (center * lax.rsqrt(spread + EPS) * gin_ref[...]).astype(BF16)

    def project(normed, weights):
        half = jnp.dot(normed, weights, preferred_element_type=F32) * 0.5
        return silu_of_half(half).astype(BF16)

    quarter = pl.ds(pl.multiple_of(h * 256, 256), 256)
    nq[...] = normalize(x_ref[quarter, :])

    cp[...] = project(normalize(cx_ref[...]), w_ref[...])
    for head in range(2):
        qall[head, 0, 0, 0, 0:CARDS, :] = cp[:, 512 + head * 128 : 640 + head * 128]
    cut = ccut_ref[...]
    row = lax.broadcasted_iota(jnp.int32, (META, 128), 0)
    told = jnp.where(row == 0, lax.shift_right_logical(cut, 8), cut & 255)
    told = jnp.where(row == 2, csurf_ref[...], told).astype(F32).astype(BF16)
    for head in range(2):
        qall[head, 0, 0, 0, CARDS:, :] = told

    pl.semaphore_wait(barrier, len(greeted))
    near, far = (at_x, at_z), (at_z, at_x)
    q_y = send(qall.at[:, 0, 0, 0], qall.at[:, 0, 0, 1], at_y())
    okay_in = [send(valid_ref, hv.at[b], at_c(b + 1)) for b in (0, 1)]

    def part(quarter_of, k):
        return pl.ds(pl.multiple_of(quarter_of * 256 + k * 128, 128), 128)

    def halo_first(k):
        return send(nq.at[pl.ds(k * 128, 128), :], hx.at[0, part(h, k), :], at_c(1))

    halo_in = {(0, 0): halo_first(0)}

    lane = lax.broadcasted_iota(jnp.int32, (CARDS, 128), 1).astype(F32)
    surf_t = jnp.transpose(hsurf_ref[...].astype(F32))
    for i in range(8):
        kf[i * 128 : i * 128 + 128, :] = jnp.where(surf_t[:, i : i + 1] == lane, 1.0, 0.0).astype(BF16)

    def only_valid(values, flags, i):
        columns = jnp.transpose(flags.astype(F32))
        okay = jnp.concatenate([columns[:, 2 * i : 2 * i + 1], columns[:, 2 * i + 1 : 2 * i + 2]], 0)
        return (values.astype(F32) * okay).astype(BF16)

    def hist_chunk(i):
        at = slice(i * CHUNK, i * CHUNK + CHUNK)
        proj = project(normalize(x_ref[at, :]), w_ref[...])
        uh[at, :] = proj[:, 0:256]
        qh[at, :] = proj[:, 512:768]
        kv[at, 0:256] = proj[:, 768:1024]
        kv[at, 256:512] = only_valid(proj[:, 256:512], valid_ref[...], i)

    hist_chunk(0)
    q_y.wait_recv()
    q_near = []
    for head in range(2):
        for d in (1, 3, 2):
            q_near.append(send(qall.at[head, 0, 0], qall.at[head, 0, d], near[head](d)))
    q_far = {(head, d): [] for head in range(2) for d in (1, 2, 3)}
    for head in range(2):
        for d in (1, 3):
            q_far[head, d].append(send(qall.at[head, 0, 0], qall.at[head, d, 0], far[head](d)))
    halo_in[0, 1] = halo_first(1)
    mine = pl.ds(pl.multiple_of(h * 256, 256), 256)
    hist_chunk(1)
    for copy in q_near:
        copy.wait_recv()
    rest = pl.ds(1, 3)
    for head in range(2):
        for d in (1, 3):
            q_far[head, d].append(
                send(qall.at[head, 0, rest], qall.at[head, d, rest], far[head](d))
            )

    halo_y, halo_core = {}, []

    def halo_pass(b, k):
        halo_in[b, k].wait_recv()
        block = hx.at[b, part(h, k), :]
        if b == 0:
            halo_in[1, k] = send(block, hx.at[1, part(h, k), :], at_c(1))
        halo_y[b, k] = send(block, block, y_peer)
        halo_core.append(send(block, block, core_peer))

    def halo_pass_on(b, k):
        halo_y[b, k].wait_recv()
        block = hx.at[b, part((h + 2) % 4, k), :]
        halo_core.append(send(block, block, core_peer))

    hist_chunk(2)
    halo_pass(0, 0)
    hist_chunk(3)
    for head in range(2):
        for d in (1, 3):
            for copy in q_far[head, d]:
                copy.wait_recv()
            pair = pl.ds(0, 2) if d == 1 else pl.ds(2, 2)
            q_far[head, 2].append(
                send(qall.at[head, d, pair], qall.at[head, 2, pair], far[head](1 if d == 1 else -1))
            )
    halo_pass(0, 1)
    into = []
    for d in (1, 2, 3):
        theirs = pl.ds(pl.multiple_of(((h + d) % 4) * 256, 256), 256)
        into.append(send(wo_ref.at[:, theirs], wc.at[mine, :], at_h(d)))
    wc[mine, :] = wo_ref[:, mine]

    def attend(queries, keys, values, mask):
        half = lax.dot_general(queries, keys, NT, preferred_element_type=F32) * HALF_SCALE
        weights = silu_of_half(half)
        if mask is not None:
            weights = jnp.where(mask(weights.shape), weights, 0.0)
        return jnp.dot(weights.astype(BF16), values, preferred_element_type=F32)

    def hist_tile(keys_ref, j, lo, hi, mask):
        ks = slice(j * CHUNK, j * CHUNK + CHUNK)
        out = []
        for head in range(2):
            a, b = head * 128, head * 128 + 128
            out.append(attend(qh[lo:hi, a:b], keys_ref[ks, a:b], keys_ref[ks, 256 + a : 256 + b], mask))
        return jnp.concatenate(out, 1)

    def not_later(shape):
        return lax.broadcasted_iota(jnp.int32, shape, 1) <= lax.broadcasted_iota(jnp.int32, shape, 0)

    start = (c * 1024).astype(F32)

    def cand_plane(head, d):
        a, b = head * 128, head * 128 + 128
        row = lax.broadcasted_iota(jnp.int32, (8, 128), 0)
        for n in range(4):
            for dy in range(2):
                told = qall[head, d, n, dy, CARDS:, :].astype(F32)
                local = told[0:1, :] * 256.0 + told[1:2, :] - start
                both = jnp.transpose(jnp.where(row == 0, local, told[2:3, :]))
                r = (n * 2 + dy) * 128
                lcb[r : r + 128, :] = jnp.broadcast_to(both[:, 0:1], (128, 128))
                qf[r : r + 128, :] = jnp.where(both[:, 1:2] == lane, 0.0, -FAR).astype(BF16)
        queries = jnp.concatenate(
            [qall[head, d, n, dy, 0:CARDS, :] for n in range(4) for dy in range(2)], 0
        )
        queries = jnp.concatenate([queries, qf[...]], 1)
        total = None
        for j in range(4):
            ks = slice(j * CHUNK, j * CHUNK + CHUNK)
            keys = jnp.concatenate([kv[ks, a:b], kf[ks, :]], 1)

            def mask(shape):
                place = (lax.broadcasted_iota(jnp.int32, shape, 1) + j * CHUNK).astype(F32)
                return place < jnp.concatenate([lcb[...], lcb[...]], 1)

            piece = attend(queries, keys, kv[ks, 256 + a : 256 + b], mask)
            total = piece if total is None else total + piece
        return total

    p_far = []

    def serve(head, d):
        pz[head, d - 1] = cand_plane(head, d).astype(BF16)
        p_far.append(send(pz.at[head, d - 1], rz.at[head, d - 1], far[head](-d)))

    def halo_project(b, i):
        at = slice(i * CHUNK, i * CHUNK + CHUNK)
        weights = jnp.concatenate([w_ref[:, 768:1024], w_ref[:, 256:512]], 1)
        proj = project(hx[b, at, :], weights)
        hkv[b, at, 0:256] = proj[:, 0:256]
        hkv[b, at, 256:512] = only_valid(proj[:, 256:512], hv[b], i)

    serve(0, 1)
    serve(1, 1)
    halo_pass_on(0, 0)
    serve(0, 3)
    serve(1, 3)
    halo_pass(1, 0)
    halo_pass_on(0, 1)
    for head in range(2):
        for copy in q_far[head, 2]:
            copy.wait_recv()
        serve(head, 2)
    halo_pass(1, 1)
    own[0] = cand_plane(0, 0)
    own[1] = cand_plane(1, 0)
    halo_pass_on(1, 0)
    attn[...] = hist_tile(kv, 0, 0, 1024, not_later)
    for j in (1, 2, 3):
        attn[j * CHUNK :, :] += hist_tile(kv, j, j * CHUNK, 1024, not_later)
    halo_pass_on(1, 1)

    for copy in p_far:
        copy.wait_recv()
    p_near = []
    for head in range(2):
        total = own[head]
        for d in (1, 2, 3):
            total += rz[head, d - 1].astype(F32)
        px[head] = total.astype(BF16)
        own[head, 0:256, :] = total[0:256]
        for d in (1, 3, 2):
            p_near.append(
                send(px.at[head, pl.ds(d * 256, 256)], rx.at[head, d - 1], near[head](-d))
            )

    full = 1024.0

    def chunk_rows(i):
        return (slice(i * CHUNK, i * CHUNK + CHUNK), CHUNK) if i < 4 else (slice(1024, 1152), CARDS)

    def stats_out(i, values):
        size = values.shape[0]
        sums = jnp.sum(values, axis=-1, keepdims=True)
        squares = jnp.sum(values * values, axis=-1, keepdims=True)
        spread = lax.broadcasted_iota(jnp.int32, (size, 128), 1)
        st[0, i, :, 0:size] = jnp.transpose(jnp.where(spread == 0, sums, squares))[0:8, :]
        return [send(st.at[0, i], st.at[d, i], at_h(d)) for d in (1, 2, 3)]

    def gate_out(i, values, update, got):
        at, size = chunk_rows(i)
        for copy in got:
            copy.wait_recv()
        both = (st[0, i] + st[1, i] + st[2, i] + st[3, i])[:, 0:size] / full
        both = jnp.transpose(both)
        mean, square = both[:, 0:1], both[:, 1:2]
        gated = (values - mean) * lax.rsqrt(square - mean * mean + EPS) * gout_ref[...] * update.astype(F32)
        gf[at, mine] = gated.astype(BF16)
        block = gf.at[at, mine]
        return [
            send(block, block, core_peer),
            send(block, block, y_peer),
        ]

    across = pl.ds(pl.multiple_of(((h + 2) % 4) * 256, 256), 256)

    def gate_forward(i, moving):
        at, _ = chunk_rows(i)
        moving[1].wait_recv()
        block = gf.at[at, across]
        moving.append(send(block, block, core_peer))

    def finish(i, moving, rows_ref, out_ref):
        at, size = chunk_rows(i)
        moving[0].wait_recv()
        moving[2].wait_recv()
        where = at if i < 4 else slice(0, CARDS)
        mixed = jnp.dot(gf[at, :], wc[...], preferred_element_type=F32)
        out_ref[where, :] = (rows_ref[where, mine].astype(F32) + mixed).astype(BF16)

    got, moving = {}, {}
    for copy in okay_in + halo_core:
        copy.wait_recv()
    for i in range(4):
        halo_project(0, i)
    for copy in p_near:
        copy.wait_recv()
    for head in range(2):
        total = own[head, 0:256, :]
        for d in (1, 2, 3):
            total += rx[head, d - 1].astype(F32)
        own[head, 0:CARDS, :] = total[0:CARDS]
        py[head] = total[CARDS:]
    p_y = send(py, ry, at_y())

    @pl.when(c >= 1)
    def _():
        for j in range(4):
            attn[...] += hist_tile(hkv.at[0], j, 0, 1024, None)

    p_y.wait_recv()
    for head in range(2):
        a, b = head * 128, head * 128 + 128
        query = cp[:, 512 + a : 512 + b].astype(F32)
        key = cp[:, 768 + a : 768 + b].astype(F32)
        half = jnp.sum(query * key, axis=-1, keepdims=True) * HALF_SCALE
        weight = silu_of_half(half).astype(BF16).astype(F32)
        term = weight * cp[:, 256 + a : 256 + b].astype(F32)
        cattn[:, a:b] = own[head, 0:CARDS, :] + ry[head] + term
    got[4] = stats_out(4, cattn[...])
    for i in range(4):
        halo_project(1, i)
    moving[4] = gate_out(4, cattn[...], cp[:, 0:256], got[4])

    for i in (3, 2, 1, 0):

        @pl.when(c >= 2)
        def _():
            def later(shape):
                return (
                    lax.broadcasted_iota(jnp.int32, shape, 1) + i * CHUNK
                    > lax.broadcasted_iota(jnp.int32, shape, 0)
                )

            hi = i * CHUNK + CHUNK
            attn[0:hi, :] += hist_tile(hkv.at[1], i, 0, hi, later)

        got[i] = stats_out(i, attn[chunk_rows(i)[0], :])

    def gate_hist(i):
        where = chunk_rows(i)[0]
        moving[i] = gate_out(i, attn[where, :], uh[where, :], got[i])

    for copy in into:
        copy.wait_recv()
    gate_hist(3)
    gate_hist(2)
    gate_forward(4, moving[4])
    gate_hist(1)
    gate_hist(0)
    gate_forward(3, moving[3])
    finish(4, moving[4], cx_ref, oc_ref)
    gate_forward(2, moving[2])
    finish(3, moving[3], x_ref, oh_ref)
    gate_forward(1, moving[1])
    finish(2, moving[2], x_ref, oh_ref)
    gate_forward(0, moving[0])
    finish(1, moving[1], x_ref, oh_ref)
    finish(0, moving[0], x_ref, oh_ref)
    for copy in sent:
        copy.wait_send()


def shards(
    history,
    candidates,
    history_valid,
    history_surface,
    candidate_surface,
    candidate_cutoff,
    gain_in,
    w_uvqk,
    gain_out,
    w_out,
):
    vmem = pl.BlockSpec(memory_space=pltpu.VMEM)
    return pl.pallas_call(
        kernel,
        out_shape=(
            jax.ShapeDtypeStruct((1024, 256), BF16),
            jax.ShapeDtypeStruct((CARDS, 256), BF16),
        ),
        in_specs=[vmem] * 10,
        out_specs=(vmem, vmem),
        scratch_shapes=[
            pltpu.VMEM((256, 1024), BF16),
            pltpu.VMEM((2, 1024, 1024), BF16),
            pltpu.VMEM((2, 8, 128), jnp.int32),
            pltpu.VMEM((1024, 512), BF16),
            pltpu.VMEM((2, 1024, 512), BF16),
            pltpu.VMEM((1024, 256), BF16),
            pltpu.VMEM((1024, 256), BF16),
            pltpu.VMEM((CARDS, 1024), BF16),
            pltpu.VMEM((1024, 128), BF16),
            pltpu.VMEM((2, 4, 4, 2, CARDS + META, 128), BF16),
            pltpu.VMEM((1024, 128), BF16),
            pltpu.VMEM((1024, 128), F32),
            pltpu.VMEM((2, 1024, 128), F32),
            pltpu.VMEM((2, 3, 1024, 128), BF16),
            pltpu.VMEM((2, 3, 1024, 128), BF16),
            pltpu.VMEM((2, 1024, 128), BF16),
            pltpu.VMEM((2, 3, 256, 128), BF16),
            pltpu.VMEM((2, CARDS, 128), F32),
            pltpu.VMEM((2, CARDS, 128), F32),
            pltpu.VMEM((1024, 256), F32),
            pltpu.VMEM((CARDS, 256), F32),
            pltpu.VMEM((4, 5, 8, 256), F32),
            pltpu.VMEM((1152, 1024), BF16),
            pltpu.VMEM((1024, 256), BF16),
            pltpu.SemaphoreType.DMA((N_SEM,)),
            pltpu.SemaphoreType.DMA((N_SEM,)),
        ],
        compiler_params=pltpu.CompilerParams(
            collective_id=0, has_side_effects=True, vmem_limit_bytes=56 * 2**20
        ),
        name="hstu",
    )(
        history,
        candidates,
        history_valid.reshape(8, 128),
        history_surface.reshape(8, 128),
        candidate_surface.reshape(1, CARDS),
        candidate_cutoff.reshape(1, CARDS),
        gain_in.reshape(1, 1024),
        w_uvqk.reshape(1024, 1024),
        gain_out.reshape(1, 256),
        w_out,
    )


def solution(mesh):
    placed = (
        P("ctx", None),
        P("ctx", None),
        P("ctx"),
        P("ctx"),
        P("ctx"),
        P("ctx"),
        P(),
        P(None, None, "cand"),
        P("cand"),
        P("cand", None),
    )
    return jax.shard_map(
        shards,
        mesh=mesh,
        in_specs=placed,
        out_specs=(P("ctx", "cand"), P("ctx", "cand")),
        check_vma=False,
    )
```

```python
import functools
import math

import jax
import jax.numpy as jnp
from jax import lax
from jax.experimental import pallas as pl
from jax.experimental.pallas import tpu as pltpu
from jax.sharding import PartitionSpec as P

HEAD = 128
EPS = 1e-05
HALF_SCALE = 0.5 / math.sqrt(HEAD)
FAR = 2.0**60
CHUNK = 256
CARDS = 128
META = 16
BF16 = jnp.bfloat16
F32 = jnp.float32
MESH = pl.DeviceIdType.MESH
NT = (((1,), (1,)), ((), ()))

N_SEM = 96


def silu_of_half(half):
    return half * jnp.tanh(half) + half


def kernel(
    x_ref, cx_ref, valid_ref, hsurf_ref, csurf_ref, ccut_ref, gin_ref, w_ref, gout_ref, wo_ref,
    oh_ref, oc_ref,
    nq, hx, hv, kv, hkv, qh, uh, cp, kf, qall, qf, lcb, own, pz, rz, px, rx, py, ry, attn, cattn, st, gf, wc,
    ssem, rsem,
):
    c = lax.axis_index("ctx")
    h = lax.axis_index("cand")
    yh, z, xx = c // 16, (c // 4) % 4, c % 4

    def at_x(d):
        return (yh * 16 + z * 4 + (xx + d + 4) % 4, h)

    def at_z(d):
        return (yh * 16 + ((z + d + 4) % 4) * 4 + xx, h)

    def at_y():
        return ((c + 16) % 32, h)

    def at_c(d):
        return ((c + d + 32) % 32, h)

    def at_h(d):
        return (c, (h + d) % 4)

    core_peer = (c, h + 1 - 2 * (h % 2))
    y_peer = (c, (h + 2) % 4)

    barrier = pltpu.get_barrier_semaphore()
    greeted = [at_h(1), at_h(2), at_h(3), at_y(), at_x(1), at_x(2), at_x(3), at_z(1), at_z(2), at_z(3)]
    greeted += [at_c(1), at_c(2), at_c(-1), at_c(-2)]
    for device in greeted:
        pl.semaphore_signal(barrier, inc=1, device_id=device, device_id_type=MESH)

    sent = []

    class Transfer:
        def __init__(self, src, dst, device, sends=None, receives=None):
            slot = len(sent)
            self.copy = pltpu.make_async_remote_copy(
                src_ref=src, dst_ref=dst, send_sem=ssem.at[slot], recv_sem=rsem.at[slot],
                device_id=device, device_id_type=MESH,
            )
            self.sends, self.receives = sends, receives
            sent.append(self)
            self.only(sends, self.copy.start)

        def only(self, condition, act):
            if condition is None:
                act()
            else:
                pl.when(condition)(lambda: act())

        def wait_recv(self):
            self.only(self.receives, self.copy.wait_recv)

        def wait_send(self):
            self.only(self.sends, self.copy.wait_send)

    send = Transfer

    def normalize(rows):
        values = rows.astype(F32)
        center = values - jnp.mean(values, axis=-1, keepdims=True)
        spread = jnp.mean(center * center, axis=-1, keepdims=True)
        return (center * lax.rsqrt(spread + EPS) * gin_ref[...]).astype(BF16)

    def project(normed, weights):
        half = jnp.dot(normed, weights, preferred_element_type=F32) * 0.5
        return silu_of_half(half).astype(BF16)

    for i in range(4):
        quarter = pl.ds(pl.multiple_of(i * CHUNK + h * 64, 64), 64)
        nq[i * 64 : i * 64 + 64, :] = normalize(x_ref[quarter, :])

    cp[...] = project(normalize(cx_ref[...]), w_ref[...])
    for head in range(2):
        qall[head, 0, 0, 0, 0:CARDS, :] = cp[:, 512 + head * 128 : 640 + head * 128]
    cut = ccut_ref[...]
    row = lax.broadcasted_iota(jnp.int32, (META, 128), 0)
    told = jnp.where(row == 0, lax.shift_right_logical(cut, 8), cut & 255)
    told = jnp.where(row == 2, csurf_ref[...], told).astype(F32).astype(BF16)
    for head in range(2):
        qall[head, 0, 0, 0, CARDS:, :] = told

    pl.semaphore_wait(barrier, len(greeted))
    near, far = (at_x, at_z), (at_z, at_x)
    q_y = send(qall.at[:, 0, 0, 0], qall.at[:, 0, 0, 1], at_y())
    okay_in = [send(valid_ref, hv.at[b], at_c(b + 1)) for b in (0, 1)]

    def part(quarter_of, i):
        return pl.ds(pl.multiple_of(i * CHUNK + quarter_of * 64, 64), 64)

    def halo_first(i):
        rows = nq.at[pl.ds(i * 64, 64), :]
        return send(rows, hx.at[0, part(h, i), :], at_c(1), c <= 30, c >= 1)

    halo_in = {(0, i): halo_first(i) for i in (3, 2, 1, 0)}
    mine = pl.ds(pl.multiple_of(h * 256, 256), 256)

    lane = lax.broadcasted_iota(jnp.int32, (CARDS, 128), 1).astype(F32)
    surf_t = jnp.transpose(hsurf_ref[...].astype(F32))
    for i in range(8):
        kf[i * 128 : i * 128 + 128, :] = jnp.where(surf_t[:, i : i + 1] == lane, 1.0, 0.0).astype(BF16)

    def only_valid(values, flags, i):
        columns = jnp.transpose(flags.astype(F32))
        okay = jnp.concatenate([columns[:, 2 * i : 2 * i + 1], columns[:, 2 * i + 1 : 2 * i + 2]], 0)
        return (values.astype(F32) * okay).astype(BF16)

    def hist_chunk(i):
        at = slice(i * CHUNK, i * CHUNK + CHUNK)
        proj = project(normalize(x_ref[at, :]), w_ref[...])
        uh[at, :] = proj[:, 0:256]
        qh[at, :] = proj[:, 512:768]
        kv[at, 0:256] = proj[:, 768:1024]
        kv[at, 256:512] = only_valid(proj[:, 256:512], valid_ref[...], i)

    hist_chunk(0)
    q_y.wait_recv()
    q_near = []
    for head in range(2):
        for d in (1, 3, 2):
            q_near.append(send(qall.at[head, 0, 0], qall.at[head, 0, d], near[head](d)))
    q_far = {(head, d): [] for head in range(2) for d in (1, 2, 3)}
    for head in range(2):
        for d in (1, 3):
            pass
    for i in (1, 2, 3):
        hist_chunk(i)
    halo_y, halo_core = {}, {}

    def halo_pass(b, i):
        halo_in[b, i].wait_recv()
        block = hx.at[b, part(h, i), :]
        known = c >= b + 1
        if b == 0:
            halo_in[1, i] = send(
                block, hx.at[1, part(h, i), :], at_c(1), (c >= 1) & (c <= 30), c >= 2
            )
        halo_y[b, i] = send(block, block, y_peer, known, known)
        halo_core[b, i] = [send(block, block, core_peer, known, known)]

    def halo_pass_on(b, i):
        halo_y[b, i].wait_recv()
        block = hx.at[b, part((h + 2) % 4, i), :]
        known = c >= b + 1
        halo_core[b, i].append(send(block, block, core_peer, known, known))

    def halo_whole(b, i):
        for copy in halo_core[b, i]:
            copy.wait_recv()

    for i in (3, 2, 1, 0):
        halo_pass(0, i)
    for copy in q_near:
        copy.wait_recv()
    for head in range(2):
        for d in (1, 3):
            q_far[head, d].append(
                send(qall.at[head, 0], qall.at[head, d], far[head](d))
            )

    def attend(queries, keys, values, mask):
        half = lax.dot_general(queries, keys, NT, preferred_element_type=F32) * HALF_SCALE
        weights = silu_of_half(half)
        if mask is not None:
            weights = jnp.where(mask(weights.shape), weights, 0.0)
        return jnp.dot(weights.astype(BF16), values, preferred_element_type=F32)

    def hist_tile(keys_ref, j, lo, hi, mask):
        ks = slice(j * CHUNK, j * CHUNK + CHUNK)
        out = []
        for head in range(2):
            a, b = head * 128, head * 128 + 128
            out.append(attend(qh[lo:hi, a:b], keys_ref[ks, a:b], keys_ref[ks, 256 + a : 256 + b], mask))
        return jnp.concatenate(out, 1)

    def not_later(shape):
        return lax.broadcasted_iota(jnp.int32, shape, 1) <= lax.broadcasted_iota(jnp.int32, shape, 0)

    start = (c * 1024).astype(F32)

    def cand_plane(head, d):
        a, b = head * 128, head * 128 + 128
        row = lax.broadcasted_iota(jnp.int32, (8, 128), 0)
        for n in range(4):
            for dy in range(2):
                told = qall[head, d, n, dy, CARDS:, :].astype(F32)
                local = told[0:1, :] * 256.0 + told[1:2, :] - start
                both = jnp.transpose(jnp.where(row == 0, local, told[2:3, :]))
                r = (n * 2 + dy) * 128
                lcb[r : r + 128, :] = jnp.broadcast_to(both[:, 0:1], (128, 128))
                qf[r : r + 128, :] = jnp.where(both[:, 1:2] == lane, 0.0, -FAR).astype(BF16)
        queries = jnp.concatenate(
            [qall[head, d, n, dy, 0:CARDS, :] for n in range(4) for dy in range(2)], 0
        )
        queries = jnp.concatenate([queries, qf[...]], 1)
        total = None
        for j in range(4):
            ks = slice(j * CHUNK, j * CHUNK + CHUNK)
            keys = jnp.concatenate([kv[ks, a:b], kf[ks, :]], 1)

            def mask(shape):
                place = (lax.broadcasted_iota(jnp.int32, shape, 1) + j * CHUNK).astype(F32)
                return place < jnp.concatenate([lcb[...], lcb[...]], 1)

            piece = attend(queries, keys, kv[ks, 256 + a : 256 + b], mask)
            total = piece if total is None else total + piece
        return total

    p_far = []

    def serve(head, d):
        pz[head, d - 1] = cand_plane(head, d).astype(BF16)
        p_far.append(send(pz.at[head, d - 1], rz.at[head, d - 1], far[head](-d)))

    def halo_project(b, i):
        at = slice(i * CHUNK, i * CHUNK + CHUNK)
        weights = jnp.concatenate([w_ref[:, 768:1024], w_ref[:, 256:512]], 1)
        proj = project(hx[b, at, :], weights)
        hkv[b, at, 0:256] = proj[:, 0:256]
        hkv[b, at, 256:512] = only_valid(proj[:, 256:512], hv[b], i)

    attn[...] = hist_tile(kv, 0, 0, 1024, not_later)
    for j in (1, 2, 3):
        attn[j * CHUNK :, :] += hist_tile(kv, j, j * CHUNK, 1024, not_later)
    own[0] = cand_plane(0, 0)
    for i in (3, 2):
        halo_pass_on(0, i)
        halo_pass(1, i)
    for i in (1, 0):
        halo_pass_on(0, i)
        halo_pass(1, i)
    for head in range(2):
        for d in (1, 3):
            for copy in q_far[head, d]:
                copy.wait_recv()
    for d, blocks in ((1, pl.ds(0, 2)), (3, pl.ds(2, 2))):
        q_far[0, 2].append(send(qall.at[0, d, blocks], qall.at[0, 2, blocks], at_z(2 - d)))
        q_far[1, 2].append(send(qall.at[1, d, blocks], qall.at[1, 2, blocks], at_x(2 - d)))
    serve(0, 1)
    serve(1, 1)
    serve(0, 3)
    serve(1, 3)
    for head in range(2):
        for copy in q_far[head, 2]:
            copy.wait_recv()
        serve(head, 2)
    for i in (3, 2, 1, 0):
        halo_pass_on(1, i)
    own[1] = cand_plane(1, 0)
    into = []
    for d in (1, 2, 3):
        theirs = pl.ds(pl.multiple_of(((h + d) % 4) * 256, 256), 256)
        into.append(send(wo_ref.at[:, theirs], wc.at[mine, :], at_h(d)))
    wc[mine, :] = wo_ref[:, mine]

    for copy in okay_in:
        copy.wait_recv()
    for i in range(4):
        halo_whole(0, i)
    for i in range(4):
        halo_project(0, i)

    @pl.when(c >= 1)
    def _():
        for j in range(4):
            attn[...] += hist_tile(hkv.at[0], j, 0, 1024, None)

    for copy in p_far:
        copy.wait_recv()
    p_near = []
    for head in range(2):
        total = own[head]
        for d in (1, 2, 3):
            total += rz[head, d - 1].astype(F32)
        px[head] = total.astype(BF16)
        own[head, 0:256, :] = total[0:256]
        for d in (1, 3, 2):
            p_near.append(
                send(px.at[head, pl.ds(d * 256, 256)], rx.at[head, d - 1], near[head](-d))
            )

    full = 1024.0

    def chunk_rows(i):
        return (slice(i * CHUNK, i * CHUNK + CHUNK), CHUNK) if i < 4 else (slice(1024, 1152), CARDS)

    def stats_out(i, values):
        size = values.shape[0]
        sums = jnp.sum(values, axis=-1, keepdims=True)
        squares = jnp.sum(values * values, axis=-1, keepdims=True)
        spread = lax.broadcasted_iota(jnp.int32, (size, 128), 1)
        st[0, i, :, 0:size] = jnp.transpose(jnp.where(spread == 0, sums, squares))[0:8, :]
        return [send(st.at[0, i], st.at[d, i], at_h(d)) for d in (1, 2, 3)]

    def gate_out(i, values, update, got):
        at, size = chunk_rows(i)
        for copy in got:
            copy.wait_recv()
        both = (st[0, i] + st[1, i] + st[2, i] + st[3, i])[:, 0:size] / full
        both = jnp.transpose(both)
        mean, square = both[:, 0:1], both[:, 1:2]
        gated = (values - mean) * lax.rsqrt(square - mean * mean + EPS) * gout_ref[...] * update.astype(F32)
        gf[at, mine] = gated.astype(BF16)
        block = gf.at[at, mine]
        return [
            send(block, block, core_peer),
            send(block, block, y_peer),
        ]

    across = pl.ds(pl.multiple_of(((h + 2) % 4) * 256, 256), 256)

    def gate_forward(i, moving):
        at, _ = chunk_rows(i)
        moving[1].wait_recv()
        block = gf.at[at, across]
        moving.append(send(block, block, core_peer))

    def finish(i, moving, rows_ref, out_ref):
        at, size = chunk_rows(i)
        moving[0].wait_recv()
        moving[2].wait_recv()
        where = at if i < 4 else slice(0, CARDS)
        mixed = jnp.dot(gf[at, :], wc[...], preferred_element_type=F32)
        out_ref[where, :] = (rows_ref[where, mine].astype(F32) + mixed).astype(BF16)

    got, moving = {}, {}
    for i in (3, 2, 1, 0):
        halo_whole(1, i)
        halo_project(1, i)

        @pl.when(c >= 2)
        def _():
            def later(shape):
                return (
                    lax.broadcasted_iota(jnp.int32, shape, 1) + i * CHUNK
                    > lax.broadcasted_iota(jnp.int32, shape, 0)
                )

            hi = i * CHUNK + CHUNK
            attn[0:hi, :] += hist_tile(hkv.at[1], i, 0, hi, later)

        got[i] = stats_out(i, attn[chunk_rows(i)[0], :])

    def gate_hist(i):
        where = chunk_rows(i)[0]
        moving[i] = gate_out(i, attn[where, :], uh[where, :], got[i])

    for copy in p_near:
        copy.wait_recv()
    for head in range(2):
        total = own[head, 0:256, :]
        for d in (1, 2, 3):
            total += rx[head, d - 1].astype(F32)
        own[head, 0:CARDS, :] = total[0:CARDS]
        py[head] = total[CARDS:]
    p_y = send(py, ry, at_y())
    gate_hist(3)
    gate_hist(2)
    selfs = []
    for head in range(2):
        a, b = head * 128, head * 128 + 128
        query = cp[:, 512 + a : 512 + b].astype(F32)
        key = cp[:, 768 + a : 768 + b].astype(F32)
        half = jnp.sum(query * key, axis=-1, keepdims=True) * HALF_SCALE
        weight = silu_of_half(half).astype(BF16).astype(F32)
        selfs.append(weight * cp[:, 256 + a : 256 + b].astype(F32))
    p_y.wait_recv()
    for head in range(2):
        a, b = head * 128, head * 128 + 128
        cattn[:, a:b] = own[head, 0:CARDS, :] + ry[head] + selfs[head]
    got[4] = stats_out(4, cattn[...])
    gate_hist(1)
    gate_hist(0)
    gate_forward(3, moving[3])
    moving[4] = gate_out(4, cattn[...], cp[:, 0:256], got[4])
    for copy in into:
        copy.wait_recv()
    gate_forward(2, moving[2])
    finish(3, moving[3], x_ref, oh_ref)
    gate_forward(1, moving[1])
    finish(2, moving[2], x_ref, oh_ref)
    gate_forward(0, moving[0])
    finish(1, moving[1], x_ref, oh_ref)
    gate_forward(4, moving[4])
    finish(0, moving[0], x_ref, oh_ref)
    finish(4, moving[4], cx_ref, oc_ref)
    for copy in sent:
        copy.wait_send()


def shards(
    history,
    candidates,
    history_valid,
    history_surface,
    candidate_surface,
    candidate_cutoff,
    gain_in,
    w_uvqk,
    gain_out,
    w_out,
):
    vmem = pl.BlockSpec(memory_space=pltpu.VMEM)
    return pl.pallas_call(
        kernel,
        out_shape=(
            jax.ShapeDtypeStruct((1024, 256), BF16),
            jax.ShapeDtypeStruct((CARDS, 256), BF16),
        ),
        in_specs=[vmem] * 10,
        out_specs=(vmem, vmem),
        scratch_shapes=[
            pltpu.VMEM((256, 1024), BF16),
            pltpu.VMEM((2, 1024, 1024), BF16),
            pltpu.VMEM((2, 8, 128), jnp.int32),
            pltpu.VMEM((1024, 512), BF16),
            pltpu.VMEM((2, 1024, 512), BF16),
            pltpu.VMEM((1024, 256), BF16),
            pltpu.VMEM((1024, 256), BF16),
            pltpu.VMEM((CARDS, 1024), BF16),
            pltpu.VMEM((1024, 128), BF16),
            pltpu.VMEM((2, 4, 4, 2, CARDS + META, 128), BF16),
            pltpu.VMEM((1024, 128), BF16),
            pltpu.VMEM((1024, 128), F32),
            pltpu.VMEM((2, 1024, 128), F32),
            pltpu.VMEM((2, 3, 1024, 128), BF16),
            pltpu.VMEM((2, 3, 1024, 128), BF16),
            pltpu.VMEM((2, 1024, 128), BF16),
            pltpu.VMEM((2, 3, 256, 128), BF16),
            pltpu.VMEM((2, CARDS, 128), F32),
            pltpu.VMEM((2, CARDS, 128), F32),
            pltpu.VMEM((1024, 256), F32),
            pltpu.VMEM((CARDS, 256), F32),
            pltpu.VMEM((4, 5, 8, 256), F32),
            pltpu.VMEM((1152, 1024), BF16),
            pltpu.VMEM((1024, 256), BF16),
            pltpu.SemaphoreType.DMA((N_SEM,)),
            pltpu.SemaphoreType.DMA((N_SEM,)),
        ],
        compiler_params=pltpu.CompilerParams(
            collective_id=0, has_side_effects=True, vmem_limit_bytes=56 * 2**20
        ),
        name="hstu",
    )(
        history,
        candidates,
        history_valid.reshape(8, 128),
        history_surface.reshape(8, 128),
        candidate_surface.reshape(1, CARDS),
        candidate_cutoff.reshape(1, CARDS),
        gain_in.reshape(1, 1024),
        w_uvqk.reshape(1024, 1024),
        gain_out.reshape(1, 256),
        w_out,
    )


def solution(mesh):
    placed = (
        P("ctx", None),
        P("ctx", None),
        P("ctx"),
        P("ctx"),
        P("ctx"),
        P("ctx"),
        P(),
        P(None, None, "cand"),
        P("cand"),
        P("cand", None),
    )
    return jax.shard_map(
        shards,
        mesh=mesh,
        in_specs=placed,
        out_specs=(P("ctx", "cand"), P("ctx", "cand")),
        check_vma=False,
    )
```

```python
import functools
import math

import jax
import jax.numpy as jnp
from jax import lax
from jax.experimental import pallas as pl
from jax.experimental.pallas import tpu as pltpu
from jax.sharding import PartitionSpec as P

HEAD = 128
EPS = 1e-05
HALF_SCALE = 0.5 / math.sqrt(HEAD)
FAR = 2.0**60
CHUNK = 256
CARDS = 128
META = 16
BF16 = jnp.bfloat16
F32 = jnp.float32
MESH = pl.DeviceIdType.MESH
NT = (((1,), (1,)), ((), ()))

N_SEM = 96


def silu_of_half(half):
    return half * jnp.tanh(half) + half


def kernel(
    x_ref, cx_ref, valid_ref, hsurf_ref, csurf_ref, ccut_ref, gin_ref, w_ref, gout_ref, wo_ref,
    oh_ref, oc_ref,
    ws, nq, hx, hv, kv, hkv, qh, uh, cp, kf, qall, qf, lcb, own, pz, rz, px, rx, py, ry, attn, cattn, st, gf, wc,
    ssem, rsem,
):
    c = lax.axis_index("ctx")
    h = lax.axis_index("cand")
    yh, z, xx = c // 16, (c // 4) % 4, c % 4

    def at_x(d):
        return (yh * 16 + z * 4 + (xx + d + 4) % 4, h)

    def at_z(d):
        return (yh * 16 + ((z + d + 4) % 4) * 4 + xx, h)

    def at_y():
        return ((c + 16) % 32, h)

    def at_c(d):
        return ((c + d + 32) % 32, h)

    def at_h(d):
        return (c, (h + d) % 4)

    core_peer = (c, h + 1 - 2 * (h % 2))
    y_peer = (c, (h + 2) % 4)

    barrier = pltpu.get_barrier_semaphore()
    greeted = [at_h(1), at_h(2), at_h(3), at_y(), at_x(1), at_x(2), at_x(3), at_z(1), at_z(2), at_z(3)]
    greeted += [at_c(1), at_c(2), at_c(-1), at_c(-2)]
    for device in greeted:
        pl.semaphore_signal(barrier, inc=1, device_id=device, device_id_type=MESH)

    sent = []

    class Transfer:
        def __init__(self, src, dst, device, sends=None, receives=None):
            slot = len(sent)
            self.copy = pltpu.make_async_remote_copy(
                src_ref=src, dst_ref=dst, send_sem=ssem.at[slot], recv_sem=rsem.at[slot],
                device_id=device, device_id_type=MESH,
            )
            self.sends, self.receives = sends, receives
            sent.append(self)
            self.only(sends, self.copy.start)

        def only(self, condition, act):
            if condition is None:
                act()
            else:
                pl.when(condition)(lambda: act())

        def wait_recv(self):
            self.only(self.receives, self.copy.wait_recv)

        def wait_send(self):
            self.only(self.sends, self.copy.wait_send)

    send = Transfer

    def normalize(rows):
        values = rows.astype(F32)
        center = values - jnp.mean(values, axis=-1, keepdims=True)
        spread = jnp.mean(center * center, axis=-1, keepdims=True)
        return (center * lax.rsqrt(spread + EPS) * gin_ref[...]).astype(BF16)

    def project(normed, weights):
        half = jnp.dot(normed, weights, preferred_element_type=F32) * 0.5
        return silu_of_half(half).astype(BF16)

    ws[...] = w_ref[...].reshape(1024, 1024)

    for i in range(4):
        quarter = pl.ds(pl.multiple_of(i * CHUNK + h * 64, 64), 64)
        nq[i * 64 : i * 64 + 64, :] = normalize(x_ref[quarter, :])

    cp[...] = project(normalize(cx_ref[...]), ws[...])
    for head in range(2):
        qall[head, 0, 0, 0, 0:CARDS, :] = cp[:, 512 + head * 128 : 640 + head * 128]
    cut = ccut_ref[...]
    row = lax.broadcasted_iota(jnp.int32, (META, 128), 0)
    told = jnp.where(row == 0, lax.shift_right_logical(cut, 8), cut & 255)
    told = jnp.where(row == 2, csurf_ref[...], told).astype(F32).astype(BF16)
    for head in range(2):
        qall[head, 0, 0, 0, CARDS:, :] = told

    pl.semaphore_wait(barrier, len(greeted))
    near, far = (at_x, at_z), (at_z, at_x)
    q_y = send(qall.at[:, 0, 0, 0], qall.at[:, 0, 0, 1], at_y())
    okay_in = [send(valid_ref, hv.at[b], at_c(b + 1)) for b in (0, 1)]

    def part(quarter_of, i):
        return pl.ds(pl.multiple_of(i * CHUNK + quarter_of * 64, 64), 64)

    def halo_first(i):
        rows = nq.at[pl.ds(i * 64, 64), :]
        return send(rows, hx.at[0, part(h, i), :], at_c(1), c <= 30, c >= 1)

    halo_in = {(0, i): halo_first(i) for i in (3, 2, 1, 0)}
    mine = pl.ds(pl.multiple_of(h * 256, 256), 256)

    lane = lax.broadcasted_iota(jnp.int32, (CARDS, 128), 1).astype(F32)
    surf_t = jnp.transpose(hsurf_ref[...].astype(F32))
    for i in range(8):
        kf[i * 128 : i * 128 + 128, :] = jnp.where(surf_t[:, i : i + 1] == lane, 1.0, 0.0).astype(BF16)

    def only_valid(values, flags, i):
        columns = jnp.transpose(flags.astype(F32))
        okay = jnp.concatenate([columns[:, 2 * i : 2 * i + 1], columns[:, 2 * i + 1 : 2 * i + 2]], 0)
        return (values.astype(F32) * okay).astype(BF16)

    def hist_chunk(i):
        at = slice(i * CHUNK, i * CHUNK + CHUNK)
        proj = project(normalize(x_ref[at, :]), ws[...])
        uh[at, :] = proj[:, 0:256]
        qh[at, :] = proj[:, 512:768]
        kv[at, 0:256] = proj[:, 768:1024]
        kv[at, 256:512] = only_valid(proj[:, 256:512], valid_ref[...], i)

    hist_chunk(0)
    q_y.wait_recv()
    q_near = []
    for head in range(2):
        for d in (1, 3, 2):
            q_near.append(send(qall.at[head, 0, 0], qall.at[head, 0, d], near[head](d)))
    q_far = {(head, d): [] for head in range(2) for d in (1, 2, 3)}
    for head in range(2):
        for d in (1, 3):
            pass
    for i in (1, 2, 3):
        hist_chunk(i)
    halo_y, halo_core = {}, {}

    def halo_pass(b, i):
        halo_in[b, i].wait_recv()
        block = hx.at[b, part(h, i), :]
        known = c >= b + 1
        if b == 0:
            halo_in[1, i] = send(
                block, hx.at[1, part(h, i), :], at_c(1), (c >= 1) & (c <= 30), c >= 2
            )
        halo_y[b, i] = send(block, block, y_peer, known, known)
        halo_core[b, i] = [send(block, block, core_peer, known, known)]

    def halo_pass_on(b, i):
        halo_y[b, i].wait_recv()
        block = hx.at[b, part((h + 2) % 4, i), :]
        known = c >= b + 1
        halo_core[b, i].append(send(block, block, core_peer, known, known))

    def halo_whole(b, i):
        for copy in halo_core[b, i]:
            copy.wait_recv()

    for i in (3, 2, 1, 0):
        halo_pass(0, i)
    for copy in q_near:
        copy.wait_recv()
    for head in range(2):
        for d in (1, 3):
            q_far[head, d].append(
                send(qall.at[head, 0], qall.at[head, d], far[head](d))
            )

    def attend(queries, keys, values, mask):
        half = lax.dot_general(queries, keys, NT, preferred_element_type=F32) * HALF_SCALE
        weights = silu_of_half(half)
        if mask is not None:
            weights = jnp.where(mask(weights.shape), weights, 0.0)
        return jnp.dot(weights.astype(BF16), values, preferred_element_type=F32)

    def hist_tile(keys_ref, j, lo, hi, mask):
        ks = slice(j * CHUNK, j * CHUNK + CHUNK)
        out = []
        for head in range(2):
            a, b = head * 128, head * 128 + 128
            out.append(attend(qh[lo:hi, a:b], keys_ref[ks, a:b], keys_ref[ks, 256 + a : 256 + b], mask))
        return jnp.concatenate(out, 1)

    def not_later(shape):
        return lax.broadcasted_iota(jnp.int32, shape, 1) <= lax.broadcasted_iota(jnp.int32, shape, 0)

    start = (c * 1024).astype(F32)

    def cand_plane(head, d):
        a, b = head * 128, head * 128 + 128
        row = lax.broadcasted_iota(jnp.int32, (8, 128), 0)
        for n in range(4):
            for dy in range(2):
                told = qall[head, d, n, dy, CARDS:, :].astype(F32)
                local = told[0:1, :] * 256.0 + told[1:2, :] - start
                both = jnp.transpose(jnp.where(row == 0, local, told[2:3, :]))
                r = (n * 2 + dy) * 128
                lcb[r : r + 128, :] = jnp.broadcast_to(both[:, 0:1], (128, 128))
                qf[r : r + 128, :] = jnp.where(both[:, 1:2] == lane, 0.0, -FAR).astype(BF16)
        queries = jnp.concatenate(
            [qall[head, d, n, dy, 0:CARDS, :] for n in range(4) for dy in range(2)], 0
        )
        queries = jnp.concatenate([queries, qf[...]], 1)
        total = None
        for j in range(4):
            ks = slice(j * CHUNK, j * CHUNK + CHUNK)
            keys = jnp.concatenate([kv[ks, a:b], kf[ks, :]], 1)

            def mask(shape):
                place = (lax.broadcasted_iota(jnp.int32, shape, 1) + j * CHUNK).astype(F32)
                return place < jnp.concatenate([lcb[...], lcb[...]], 1)

            piece = attend(queries, keys, kv[ks, 256 + a : 256 + b], mask)
            total = piece if total is None else total + piece
        return total

    p_far = []

    def serve(head, d):
        pz[head, d - 1] = cand_plane(head, d).astype(BF16)
        p_far.append(send(pz.at[head, d - 1], rz.at[head, d - 1], far[head](-d)))

    def halo_project(b, i):
        at = slice(i * CHUNK, i * CHUNK + CHUNK)
        weights = jnp.concatenate([ws[:, 768:1024], ws[:, 256:512]], 1)
        proj = project(hx[b, at, :], weights)
        hkv[b, at, 0:256] = proj[:, 0:256]
        hkv[b, at, 256:512] = only_valid(proj[:, 256:512], hv[b], i)

    attn[...] = hist_tile(kv, 0, 0, 1024, not_later)
    for j in (1, 2, 3):
        attn[j * CHUNK :, :] += hist_tile(kv, j, j * CHUNK, 1024, not_later)
    own[0] = cand_plane(0, 0)
    for i in (3, 2):
        halo_pass_on(0, i)
        halo_pass(1, i)
    for i in (1, 0):
        halo_pass_on(0, i)
        halo_pass(1, i)
    for head in range(2):
        for d in (1, 3):
            for copy in q_far[head, d]:
                copy.wait_recv()
    for d, blocks in ((1, pl.ds(0, 2)), (3, pl.ds(2, 2))):
        q_far[0, 2].append(send(qall.at[0, d, blocks], qall.at[0, 2, blocks], at_z(2 - d)))
        q_far[1, 2].append(send(qall.at[1, d, blocks], qall.at[1, 2, blocks], at_x(2 - d)))
    serve(0, 1)
    serve(1, 1)
    serve(0, 3)
    serve(1, 3)
    for head in range(2):
        for copy in q_far[head, 2]:
            copy.wait_recv()
        serve(head, 2)
    for i in (3, 2, 1, 0):
        halo_pass_on(1, i)
    own[1] = cand_plane(1, 0)
    into = []
    for d in (1, 2, 3):
        theirs = pl.ds(pl.multiple_of(((h + d) % 4) * 256, 256), 256)
        into.append(send(wo_ref.at[:, theirs], wc.at[mine, :], at_h(d)))
    wc[mine, :] = wo_ref[:, mine]

    for copy in okay_in:
        copy.wait_recv()
    for i in range(4):
        halo_whole(0, i)
    for i in range(4):
        halo_project(0, i)

    @pl.when(c >= 1)
    def _():
        for j in range(4):
            attn[...] += hist_tile(hkv.at[0], j, 0, 1024, None)

    for copy in p_far:
        copy.wait_recv()
    p_near = []
    for head in range(2):
        total = own[head]
        for d in (1, 2, 3):
            total += rz[head, d - 1].astype(F32)
        px[head] = total.astype(BF16)
        own[head, 0:256, :] = total[0:256]
        for d in (1, 3, 2):
            p_near.append(
                send(px.at[head, pl.ds(d * 256, 256)], rx.at[head, d - 1], near[head](-d))
            )

    full = 1024.0

    def chunk_rows(i):
        return (slice(i * CHUNK, i * CHUNK + CHUNK), CHUNK) if i < 4 else (slice(1024, 1152), CARDS)

    def stats_out(i, values):
        size = values.shape[0]
        sums = jnp.sum(values, axis=-1, keepdims=True)
        squares = jnp.sum(values * values, axis=-1, keepdims=True)
        spread = lax.broadcasted_iota(jnp.int32, (size, 128), 1)
        st[0, i, :, 0:size] = jnp.transpose(jnp.where(spread == 0, sums, squares))[0:8, :]
        return [send(st.at[0, i], st.at[d, i], at_h(d)) for d in (1, 2, 3)]

    def gate_out(i, values, update, got):
        at, size = chunk_rows(i)
        for copy in got:
            copy.wait_recv()
        both = (st[0, i] + st[1, i] + st[2, i] + st[3, i])[:, 0:size] / full
        both = jnp.transpose(both)
        mean, square = both[:, 0:1], both[:, 1:2]
        gated = (values - mean) * lax.rsqrt(square - mean * mean + EPS) * gout_ref[...] * update.astype(F32)
        gf[at, mine] = gated.astype(BF16)
        block = gf.at[at, mine]
        return [
            send(block, block, core_peer),
            send(block, block, y_peer),
        ]

    across = pl.ds(pl.multiple_of(((h + 2) % 4) * 256, 256), 256)

    def gate_forward(i, moving):
        at, _ = chunk_rows(i)
        moving[1].wait_recv()
        block = gf.at[at, across]
        moving.append(send(block, block, core_peer))

    def finish(i, moving, rows_ref, out_ref):
        at, size = chunk_rows(i)
        moving[0].wait_recv()
        moving[2].wait_recv()
        where = at if i < 4 else slice(0, CARDS)
        mixed = jnp.dot(gf[at, :], wc[...], preferred_element_type=F32)
        out_ref[where, :] = (rows_ref[where, mine].astype(F32) + mixed).astype(BF16)

    got, moving = {}, {}
    for i in (3, 2, 1, 0):
        halo_whole(1, i)
        halo_project(1, i)

        @pl.when(c >= 2)
        def _():
            def later(shape):
                return (
                    lax.broadcasted_iota(jnp.int32, shape, 1) + i * CHUNK
                    > lax.broadcasted_iota(jnp.int32, shape, 0)
                )

            hi = i * CHUNK + CHUNK
            attn[0:hi, :] += hist_tile(hkv.at[1], i, 0, hi, later)

        got[i] = stats_out(i, attn[chunk_rows(i)[0], :])

    def gate_hist(i):
        where = chunk_rows(i)[0]
        moving[i] = gate_out(i, attn[where, :], uh[where, :], got[i])

    for copy in p_near:
        copy.wait_recv()
    for head in range(2):
        total = own[head, 0:256, :]
        for d in (1, 2, 3):
            total += rx[head, d - 1].astype(F32)
        own[head, 0:CARDS, :] = total[0:CARDS]
        py[head] = total[CARDS:]
    p_y = send(py, ry, at_y())
    gate_hist(3)
    gate_hist(2)
    selfs = []
    for head in range(2):
        a, b = head * 128, head * 128 + 128
        query = cp[:, 512 + a : 512 + b].astype(F32)
        key = cp[:, 768 + a : 768 + b].astype(F32)
        half = jnp.sum(query * key, axis=-1, keepdims=True) * HALF_SCALE
        weight = silu_of_half(half).astype(BF16).astype(F32)
        selfs.append(weight * cp[:, 256 + a : 256 + b].astype(F32))
    p_y.wait_recv()
    for head in range(2):
        a, b = head * 128, head * 128 + 128
        cattn[:, a:b] = own[head, 0:CARDS, :] + ry[head] + selfs[head]
    got[4] = stats_out(4, cattn[...])
    gate_hist(1)
    gate_hist(0)
    gate_forward(3, moving[3])
    moving[4] = gate_out(4, cattn[...], cp[:, 0:256], got[4])
    for copy in into:
        copy.wait_recv()
    gate_forward(2, moving[2])
    finish(3, moving[3], x_ref, oh_ref)
    gate_forward(1, moving[1])
    finish(2, moving[2], x_ref, oh_ref)
    gate_forward(0, moving[0])
    finish(1, moving[1], x_ref, oh_ref)
    gate_forward(4, moving[4])
    finish(0, moving[0], x_ref, oh_ref)
    finish(4, moving[4], cx_ref, oc_ref)
    for copy in sent:
        copy.wait_send()


def shards(
    history,
    candidates,
    history_valid,
    history_surface,
    candidate_surface,
    candidate_cutoff,
    gain_in,
    w_uvqk,
    gain_out,
    w_out,
):
    vmem = pl.BlockSpec(memory_space=pltpu.VMEM)
    return pl.pallas_call(
        kernel,
        out_shape=(
            jax.ShapeDtypeStruct((1024, 256), BF16),
            jax.ShapeDtypeStruct((CARDS, 256), BF16),
        ),
        in_specs=[vmem] * 10,
        out_specs=(vmem, vmem),
        scratch_shapes=[
            pltpu.VMEM((1024, 1024), BF16),
            pltpu.VMEM((256, 1024), BF16),
            pltpu.VMEM((2, 1024, 1024), BF16),
            pltpu.VMEM((2, 8, 128), jnp.int32),
            pltpu.VMEM((1024, 512), BF16),
            pltpu.VMEM((2, 1024, 512), BF16),
            pltpu.VMEM((1024, 256), BF16),
            pltpu.VMEM((1024, 256), BF16),
            pltpu.VMEM((CARDS, 1024), BF16),
            pltpu.VMEM((1024, 128), BF16),
            pltpu.VMEM((2, 4, 4, 2, CARDS + META, 128), BF16),
            pltpu.VMEM((1024, 128), BF16),
            pltpu.VMEM((1024, 128), F32),
            pltpu.VMEM((2, 1024, 128), F32),
            pltpu.VMEM((2, 3, 1024, 128), BF16),
            pltpu.VMEM((2, 3, 1024, 128), BF16),
            pltpu.VMEM((2, 1024, 128), BF16),
            pltpu.VMEM((2, 3, 256, 128), BF16),
            pltpu.VMEM((2, CARDS, 128), F32),
            pltpu.VMEM((2, CARDS, 128), F32),
            pltpu.VMEM((1024, 256), F32),
            pltpu.VMEM((CARDS, 256), F32),
            pltpu.VMEM((4, 5, 8, 256), F32),
            pltpu.VMEM((1152, 1024), BF16),
            pltpu.VMEM((1024, 256), BF16),
            pltpu.SemaphoreType.DMA((N_SEM,)),
            pltpu.SemaphoreType.DMA((N_SEM,)),
        ],
        compiler_params=pltpu.CompilerParams(
            collective_id=0, has_side_effects=True, vmem_limit_bytes=56 * 2**20
        ),
        name="hstu",
    )(
        history,
        candidates,
        history_valid.reshape(8, 128),
        history_surface.reshape(8, 128),
        candidate_surface.reshape(1, CARDS),
        candidate_cutoff.reshape(1, CARDS),
        gain_in.reshape(1, 1024),
        w_uvqk,
        gain_out.reshape(1, 256),
        w_out,
    )


def solution(mesh):
    placed = (
        P("ctx", None),
        P("ctx", None),
        P("ctx"),
        P("ctx"),
        P("ctx"),
        P("ctx"),
        P(),
        P(None, None, "cand"),
        P("cand"),
        P("cand", None),
    )
    return jax.shard_map(
        shards,
        mesh=mesh,
        in_specs=placed,
        out_specs=(P("ctx", "cand"), P("ctx", "cand")),
        check_vma=False,
    )
```

```python
import functools
import math

import jax
import jax.numpy as jnp
from jax import lax
from jax.experimental import pallas as pl
from jax.experimental.pallas import tpu as pltpu
from jax.sharding import PartitionSpec as P

HEAD = 128
EPS = 1e-05
HALF_SCALE = 0.5 / math.sqrt(HEAD)
FAR = 2.0**60
CHUNK = 256
CARDS = 128
META = 16
BF16 = jnp.bfloat16
F32 = jnp.float32
MESH = pl.DeviceIdType.MESH
NT = (((1,), (1,)), ((), ()))

N_SEM = 96


def silu_of_half(half):
    return half * jnp.tanh(half) + half


def kernel(
    x_hbm, cx_ref, valid_ref, hsurf_ref, csurf_ref, ccut_ref, gin_ref, w_hbm, gout_ref, wo_hbm,
    oh_ref, oc_ref,
    x_ref, w_ref, wo_ref, ws, nq, hx, hv, kv, hkv, qh, uh, cp, kf, qall, qf, lcb, own, pz, rz, px, rx, py, ry, attn, cattn, st, gf, wc,
    ssem, rsem, lsem,
):
    c = lax.axis_index("ctx")
    h = lax.axis_index("cand")
    yh, z, xx = c // 16, (c // 4) % 4, c % 4

    def at_x(d):
        return (yh * 16 + z * 4 + (xx + d + 4) % 4, h)

    def at_z(d):
        return (yh * 16 + ((z + d + 4) % 4) * 4 + xx, h)

    def at_y():
        return ((c + 16) % 32, h)

    def at_c(d):
        return ((c + d + 32) % 32, h)

    def at_h(d):
        return (c, (h + d) % 4)

    core_peer = (c, h + 1 - 2 * (h % 2))
    y_peer = (c, (h + 2) % 4)

    barrier = pltpu.get_barrier_semaphore()
    greeted = [at_h(1), at_h(2), at_h(3), at_y(), at_x(1), at_x(2), at_x(3), at_z(1), at_z(2), at_z(3)]
    greeted += [at_c(1), at_c(2), at_c(-1), at_c(-2)]
    for device in greeted:
        pl.semaphore_signal(barrier, inc=1, device_id=device, device_id_type=MESH)

    loads = [
        pltpu.make_async_copy(src, dst, lsem.at[i])
        for i, (src, dst) in enumerate([(w_hbm, w_ref), (x_hbm, x_ref), (wo_hbm, wo_ref)])
    ]
    for load in loads:
        load.start()
    sent = []

    class Transfer:
        def __init__(self, src, dst, device, sends=None, receives=None):
            slot = len(sent)
            self.copy = pltpu.make_async_remote_copy(
                src_ref=src, dst_ref=dst, send_sem=ssem.at[slot], recv_sem=rsem.at[slot],
                device_id=device, device_id_type=MESH,
            )
            self.sends, self.receives = sends, receives
            sent.append(self)
            self.only(sends, self.copy.start)

        def only(self, condition, act):
            if condition is None:
                act()
            else:
                pl.when(condition)(lambda: act())

        def wait_recv(self):
            self.only(self.receives, self.copy.wait_recv)

        def wait_send(self):
            self.only(self.sends, self.copy.wait_send)

    send = Transfer

    def normalize(rows):
        values = rows.astype(F32)
        center = values - jnp.mean(values, axis=-1, keepdims=True)
        spread = jnp.mean(center * center, axis=-1, keepdims=True)
        return (center * lax.rsqrt(spread + EPS) * gin_ref[...]).astype(BF16)

    def project(normed, weights):
        half = jnp.dot(normed, weights, preferred_element_type=F32) * 0.5
        return silu_of_half(half).astype(BF16)

    loads[0].wait()
    ws[...] = w_ref[...].reshape(1024, 1024)
    loads[1].wait()
    loads[2].wait()

    for i in range(4):
        quarter = pl.ds(pl.multiple_of(i * CHUNK + h * 64, 64), 64)
        nq[i * 64 : i * 64 + 64, :] = normalize(x_ref[quarter, :])

    cp[...] = project(normalize(cx_ref[...]), ws[...])
    for head in range(2):
        qall[head, 0, 0, 0, 0:CARDS, :] = cp[:, 512 + head * 128 : 640 + head * 128]
    cut = ccut_ref[...]
    row = lax.broadcasted_iota(jnp.int32, (META, 128), 0)
    told = jnp.where(row == 0, lax.shift_right_logical(cut, 8), cut & 255)
    told = jnp.where(row == 2, csurf_ref[...], told).astype(F32).astype(BF16)
    for head in range(2):
        qall[head, 0, 0, 0, CARDS:, :] = told

    pl.semaphore_wait(barrier, len(greeted))
    near, far = (at_x, at_z), (at_z, at_x)
    q_y = send(qall.at[:, 0, 0, 0], qall.at[:, 0, 0, 1], at_y())
    okay_in = [send(valid_ref, hv.at[b], at_c(b + 1)) for b in (0, 1)]

    def part(quarter_of, i):
        return pl.ds(pl.multiple_of(i * CHUNK + quarter_of * 64, 64), 64)

    def halo_first(i):
        rows = nq.at[pl.ds(i * 64, 64), :]
        return send(rows, hx.at[0, part(h, i), :], at_c(1), c <= 30, c >= 1)

    halo_in = {(0, i): halo_first(i) for i in (3, 2, 1, 0)}
    mine = pl.ds(pl.multiple_of(h * 256, 256), 256)

    lane = lax.broadcasted_iota(jnp.int32, (CARDS, 128), 1).astype(F32)
    surf_t = jnp.transpose(hsurf_ref[...].astype(F32))
    for i in range(8):
        kf[i * 128 : i * 128 + 128, :] = jnp.where(surf_t[:, i : i + 1] == lane, 1.0, 0.0).astype(BF16)

    def only_valid(values, flags, i):
        columns = jnp.transpose(flags.astype(F32))
        okay = jnp.concatenate([columns[:, 2 * i : 2 * i + 1], columns[:, 2 * i + 1 : 2 * i + 2]], 0)
        return (values.astype(F32) * okay).astype(BF16)

    def hist_chunk(i):
        at = slice(i * CHUNK, i * CHUNK + CHUNK)
        proj = project(normalize(x_ref[at, :]), ws[...])
        uh[at, :] = proj[:, 0:256]
        qh[at, :] = proj[:, 512:768]
        kv[at, 0:256] = proj[:, 768:1024]
        kv[at, 256:512] = only_valid(proj[:, 256:512], valid_ref[...], i)

    hist_chunk(0)
    q_y.wait_recv()
    q_near = []
    for head in range(2):
        for d in (1, 3, 2):
            q_near.append(send(qall.at[head, 0, 0], qall.at[head, 0, d], near[head](d)))
    q_far = {(head, d): [] for head in range(2) for d in (1, 2, 3)}
    for head in range(2):
        for d in (1, 3):
            pass
    for i in (1, 2, 3):
        hist_chunk(i)
    halo_y, halo_core = {}, {}

    def halo_pass(b, i):
        halo_in[b, i].wait_recv()
        block = hx.at[b, part(h, i), :]
        known = c >= b + 1
        if b == 0:
            halo_in[1, i] = send(
                block, hx.at[1, part(h, i), :], at_c(1), (c >= 1) & (c <= 30), c >= 2
            )
        halo_y[b, i] = send(block, block, y_peer, known, known)
        halo_core[b, i] = [send(block, block, core_peer, known, known)]

    def halo_pass_on(b, i):
        halo_y[b, i].wait_recv()
        block = hx.at[b, part((h + 2) % 4, i), :]
        known = c >= b + 1
        halo_core[b, i].append(send(block, block, core_peer, known, known))

    def halo_whole(b, i):
        for copy in halo_core[b, i]:
            copy.wait_recv()

    for i in (3, 2, 1, 0):
        halo_pass(0, i)
    for copy in q_near:
        copy.wait_recv()
    for head in range(2):
        for d in (1, 3):
            q_far[head, d].append(
                send(qall.at[head, 0], qall.at[head, d], far[head](d))
            )

    def attend(queries, keys, values, mask):
        half = lax.dot_general(queries, keys, NT, preferred_element_type=F32) * HALF_SCALE
        weights = silu_of_half(half)
        if mask is not None:
            weights = jnp.where(mask(weights.shape), weights, 0.0)
        return jnp.dot(weights.astype(BF16), values, preferred_element_type=F32)

    def hist_tile(keys_ref, j, lo, hi, mask):
        ks = slice(j * CHUNK, j * CHUNK + CHUNK)
        out = []
        for head in range(2):
            a, b = head * 128, head * 128 + 128
            out.append(attend(qh[lo:hi, a:b], keys_ref[ks, a:b], keys_ref[ks, 256 + a : 256 + b], mask))
        return jnp.concatenate(out, 1)

    def not_later(shape):
        return lax.broadcasted_iota(jnp.int32, shape, 1) <= lax.broadcasted_iota(jnp.int32, shape, 0)

    start = (c * 1024).astype(F32)

    def cand_plane(head, d):
        a, b = head * 128, head * 128 + 128
        row = lax.broadcasted_iota(jnp.int32, (8, 128), 0)
        for n in range(4):
            for dy in range(2):
                told = qall[head, d, n, dy, CARDS:, :].astype(F32)
                local = told[0:1, :] * 256.0 + told[1:2, :] - start
                both = jnp.transpose(jnp.where(row == 0, local, told[2:3, :]))
                r = (n * 2 + dy) * 128
                lcb[r : r + 128, :] = jnp.broadcast_to(both[:, 0:1], (128, 128))
                qf[r : r + 128, :] = jnp.where(both[:, 1:2] == lane, 0.0, -FAR).astype(BF16)
        queries = jnp.concatenate(
            [qall[head, d, n, dy, 0:CARDS, :] for n in range(4) for dy in range(2)], 0
        )
        queries = jnp.concatenate([queries, qf[...]], 1)
        total = None
        for j in range(4):
            ks = slice(j * CHUNK, j * CHUNK + CHUNK)
            keys = jnp.concatenate([kv[ks, a:b], kf[ks, :]], 1)

            def mask(shape):
                place = (lax.broadcasted_iota(jnp.int32, shape, 1) + j * CHUNK).astype(F32)
                return place < jnp.concatenate([lcb[...], lcb[...]], 1)

            piece = attend(queries, keys, kv[ks, 256 + a : 256 + b], mask)
            total = piece if total is None else total + piece
        return total

    p_far = []

    def serve(head, d):
        pz[head, d - 1] = cand_plane(head, d).astype(BF16)
        p_far.append(send(pz.at[head, d - 1], rz.at[head, d - 1], far[head](-d)))

    def halo_project(b, i):
        at = slice(i * CHUNK, i * CHUNK + CHUNK)
        weights = jnp.concatenate([ws[:, 768:1024], ws[:, 256:512]], 1)
        proj = project(hx[b, at, :], weights)
        hkv[b, at, 0:256] = proj[:, 0:256]
        hkv[b, at, 256:512] = only_valid(proj[:, 256:512], hv[b], i)

    attn[...] = hist_tile(kv, 0, 0, 1024, not_later)
    for j in (1, 2, 3):
        attn[j * CHUNK :, :] += hist_tile(kv, j, j * CHUNK, 1024, not_later)
    own[0] = cand_plane(0, 0)
    for i in (3, 2):
        halo_pass_on(0, i)
        halo_pass(1, i)
    for i in (1, 0):
        halo_pass_on(0, i)
        halo_pass(1, i)
    for head in range(2):
        for d in (1, 3):
            for copy in q_far[head, d]:
                copy.wait_recv()
    for d, blocks in ((1, pl.ds(0, 2)), (3, pl.ds(2, 2))):
        q_far[0, 2].append(send(qall.at[0, d, blocks], qall.at[0, 2, blocks], at_z(2 - d)))
        q_far[1, 2].append(send(qall.at[1, d, blocks], qall.at[1, 2, blocks], at_x(2 - d)))
    serve(0, 1)
    serve(1, 1)
    serve(0, 3)
    serve(1, 3)
    for head in range(2):
        for copy in q_far[head, 2]:
            copy.wait_recv()
        serve(head, 2)
    for i in (3, 2, 1, 0):
        halo_pass_on(1, i)
    own[1] = cand_plane(1, 0)
    into = []
    for d in (1, 2, 3):
        theirs = pl.ds(pl.multiple_of(((h + d) % 4) * 256, 256), 256)
        into.append(send(wo_ref.at[:, theirs], wc.at[mine, :], at_h(d)))
    wc[mine, :] = wo_ref[:, mine]

    for copy in okay_in:
        copy.wait_recv()
    for i in range(4):
        halo_whole(0, i)
    for i in range(4):
        halo_project(0, i)

    @pl.when(c >= 1)
    def _():
        for j in range(4):
            attn[...] += hist_tile(hkv.at[0], j, 0, 1024, None)

    for copy in p_far:
        copy.wait_recv()
    p_near = []
    for head in range(2):
        total = own[head]
        for d in (1, 2, 3):
            total += rz[head, d - 1].astype(F32)
        px[head] = total.astype(BF16)
        own[head, 0:256, :] = total[0:256]
        for d in (1, 3, 2):
            p_near.append(
                send(px.at[head, pl.ds(d * 256, 256)], rx.at[head, d - 1], near[head](-d))
            )

    full = 1024.0

    def chunk_rows(i):
        return (slice(i * CHUNK, i * CHUNK + CHUNK), CHUNK) if i < 4 else (slice(1024, 1152), CARDS)

    def stats_out(i, values):
        size = values.shape[0]
        sums = jnp.sum(values, axis=-1, keepdims=True)
        squares = jnp.sum(values * values, axis=-1, keepdims=True)
        spread = lax.broadcasted_iota(jnp.int32, (size, 128), 1)
        st[0, i, :, 0:size] = jnp.transpose(jnp.where(spread == 0, sums, squares))[0:8, :]
        return [send(st.at[0, i], st.at[d, i], at_h(d)) for d in (1, 2, 3)]

    def gate_out(i, values, update, got):
        at, size = chunk_rows(i)
        for copy in got:
            copy.wait_recv()
        both = (st[0, i] + st[1, i] + st[2, i] + st[3, i])[:, 0:size] / full
        both = jnp.transpose(both)
        mean, square = both[:, 0:1], both[:, 1:2]
        gated = (values - mean) * lax.rsqrt(square - mean * mean + EPS) * gout_ref[...] * update.astype(F32)
        gf[at, mine] = gated.astype(BF16)
        block = gf.at[at, mine]
        return [
            send(block, block, core_peer),
            send(block, block, y_peer),
        ]

    across = pl.ds(pl.multiple_of(((h + 2) % 4) * 256, 256), 256)

    def gate_forward(i, moving):
        at, _ = chunk_rows(i)
        moving[1].wait_recv()
        block = gf.at[at, across]
        moving.append(send(block, block, core_peer))

    def finish(i, moving, rows_ref, out_ref):
        at, size = chunk_rows(i)
        moving[0].wait_recv()
        moving[2].wait_recv()
        where = at if i < 4 else slice(0, CARDS)
        mixed = jnp.dot(gf[at, :], wc[...], preferred_element_type=F32)
        out_ref[where, :] = (rows_ref[where, mine].astype(F32) + mixed).astype(BF16)

    got, moving = {}, {}
    for i in (3, 2, 1, 0):
        halo_whole(1, i)
        halo_project(1, i)

        @pl.when(c >= 2)
        def _():
            def later(shape):
                return (
                    lax.broadcasted_iota(jnp.int32, shape, 1) + i * CHUNK
                    > lax.broadcasted_iota(jnp.int32, shape, 0)
                )

            hi = i * CHUNK + CHUNK
            attn[0:hi, :] += hist_tile(hkv.at[1], i, 0, hi, later)

        got[i] = stats_out(i, attn[chunk_rows(i)[0], :])

    def gate_hist(i):
        where = chunk_rows(i)[0]
        moving[i] = gate_out(i, attn[where, :], uh[where, :], got[i])

    for copy in p_near:
        copy.wait_recv()
    for head in range(2):
        total = own[head, 0:256, :]
        for d in (1, 2, 3):
            total += rx[head, d - 1].astype(F32)
        own[head, 0:CARDS, :] = total[0:CARDS]
        py[head] = total[CARDS:]
    p_y = send(py, ry, at_y())
    gate_hist(3)
    gate_hist(2)
    selfs = []
    for head in range(2):
        a, b = head * 128, head * 128 + 128
        query = cp[:, 512 + a : 512 + b].astype(F32)
        key = cp[:, 768 + a : 768 + b].astype(F32)
        half = jnp.sum(query * key, axis=-1, keepdims=True) * HALF_SCALE
        weight = silu_of_half(half).astype(BF16).astype(F32)
        selfs.append(weight * cp[:, 256 + a : 256 + b].astype(F32))
    p_y.wait_recv()
    for head in range(2):
        a, b = head * 128, head * 128 + 128
        cattn[:, a:b] = own[head, 0:CARDS, :] + ry[head] + selfs[head]
    got[4] = stats_out(4, cattn[...])
    gate_hist(1)
    gate_hist(0)
    gate_forward(3, moving[3])
    moving[4] = gate_out(4, cattn[...], cp[:, 0:256], got[4])
    for copy in into:
        copy.wait_recv()
    gate_forward(2, moving[2])
    finish(3, moving[3], x_ref, oh_ref)
    gate_forward(1, moving[1])
    finish(2, moving[2], x_ref, oh_ref)
    gate_forward(0, moving[0])
    finish(1, moving[1], x_ref, oh_ref)
    gate_forward(4, moving[4])
    finish(0, moving[0], x_ref, oh_ref)
    finish(4, moving[4], cx_ref, oc_ref)
    for copy in sent:
        copy.wait_send()


def shards(
    history,
    candidates,
    history_valid,
    history_surface,
    candidate_surface,
    candidate_cutoff,
    gain_in,
    w_uvqk,
    gain_out,
    w_out,
):
    vmem = pl.BlockSpec(memory_space=pltpu.VMEM)
    hbm = pl.BlockSpec(memory_space=pl.ANY)
    return pl.pallas_call(
        kernel,
        out_shape=(
            jax.ShapeDtypeStruct((1024, 256), BF16),
            jax.ShapeDtypeStruct((CARDS, 256), BF16),
        ),
        in_specs=[hbm] + [vmem] * 6 + [hbm, vmem, hbm],
        out_specs=(vmem, vmem),
        scratch_shapes=[
            pltpu.VMEM((1024, 1024), BF16),
            pltpu.VMEM((1024, 4, 256), BF16),
            pltpu.VMEM((256, 1024), BF16),
            pltpu.VMEM((1024, 1024), BF16),
            pltpu.VMEM((256, 1024), BF16),
            pltpu.VMEM((2, 1024, 1024), BF16),
            pltpu.VMEM((2, 8, 128), jnp.int32),
            pltpu.VMEM((1024, 512), BF16),
            pltpu.VMEM((2, 1024, 512), BF16),
            pltpu.VMEM((1024, 256), BF16),
            pltpu.VMEM((1024, 256), BF16),
            pltpu.VMEM((CARDS, 1024), BF16),
            pltpu.VMEM((1024, 128), BF16),
            pltpu.VMEM((2, 4, 4, 2, CARDS + META, 128), BF16),
            pltpu.VMEM((1024, 128), BF16),
            pltpu.VMEM((1024, 128), F32),
            pltpu.VMEM((2, 1024, 128), F32),
            pltpu.VMEM((2, 3, 1024, 128), BF16),
            pltpu.VMEM((2, 3, 1024, 128), BF16),
            pltpu.VMEM((2, 1024, 128), BF16),
            pltpu.VMEM((2, 3, 256, 128), BF16),
            pltpu.VMEM((2, CARDS, 128), F32),
            pltpu.VMEM((2, CARDS, 128), F32),
            pltpu.VMEM((1024, 256), F32),
            pltpu.VMEM((CARDS, 256), F32),
            pltpu.VMEM((4, 5, 8, 256), F32),
            pltpu.VMEM((1152, 1024), BF16),
            pltpu.VMEM((1024, 256), BF16),
            pltpu.SemaphoreType.DMA((N_SEM,)),
            pltpu.SemaphoreType.DMA((N_SEM,)),
            pltpu.SemaphoreType.DMA((3,)),
        ],
        compiler_params=pltpu.CompilerParams(
            collective_id=0, has_side_effects=True, vmem_limit_bytes=56 * 2**20
        ),
        name="hstu",
    )(
        history,
        candidates,
        history_valid.reshape(8, 128),
        history_surface.reshape(8, 128),
        candidate_surface.reshape(1, CARDS),
        candidate_cutoff.reshape(1, CARDS),
        gain_in.reshape(1, 1024),
        w_uvqk,
        gain_out.reshape(1, 256),
        w_out,
    )


def solution(mesh):
    placed = (
        P("ctx", None),
        P("ctx", None),
        P("ctx"),
        P("ctx"),
        P("ctx"),
        P("ctx"),
        P(),
        P(None, None, "cand"),
        P("cand"),
        P("cand", None),
    )
    return jax.shard_map(
        shards,
        mesh=mesh,
        in_specs=placed,
        out_specs=(P("ctx", "cand"), P("ctx", "cand")),
        check_vma=False,
    )
```

```python
import functools
import math

import jax
import jax.numpy as jnp
from jax import lax
from jax.experimental import pallas as pl
from jax.experimental.pallas import tpu as pltpu
from jax.sharding import PartitionSpec as P

HEAD = 128
EPS = 1e-05
HALF_SCALE = 0.5 / math.sqrt(HEAD)
FAR = 2.0**60
CHUNK = 256
CARDS = 128
META = 16
BF16 = jnp.bfloat16
F32 = jnp.float32
MESH = pl.DeviceIdType.MESH
NT = (((1,), (1,)), ((), ()))

N_SEM = 96


def silu_of_half(half):
    return half * jnp.tanh(half) + half


def kernel(
    x_hbm, cx_ref, valid_ref, hsurf_ref, csurf_ref, ccut_ref, gin_ref, w_hbm, gout_ref, wo_hbm,
    oh_ref, oc_ref,
    x_ref, w_ref, wo_ref, ws, nq, hx, hv, kv, hkv, qh, uh, cp, kf, qall, qf, lcb, own, pz, rz, px, rx, py, ry, attn, cattn, st, gf, wc,
    ssem, rsem, lsem,
):
    c = lax.axis_index("ctx")
    h = lax.axis_index("cand")
    yh, z, xx = c // 16, (c // 4) % 4, c % 4

    def at_x(d):
        return (yh * 16 + z * 4 + (xx + d + 4) % 4, h)

    def at_z(d):
        return (yh * 16 + ((z + d + 4) % 4) * 4 + xx, h)

    def at_y():
        return ((c + 16) % 32, h)

    def at_c(d):
        return ((c + d + 32) % 32, h)

    def at_h(d):
        return (c, (h + d) % 4)

    core_peer = (c, h + 1 - 2 * (h % 2))
    y_peer = (c, (h + 2) % 4)

    barrier = pltpu.get_barrier_semaphore()
    greeted = [at_h(1), at_h(2), at_h(3), at_y(), at_x(1), at_x(2), at_x(3), at_z(1), at_z(2), at_z(3)]
    greeted += [at_c(1), at_c(2), at_c(-1), at_c(-2)]
    for device in greeted:
        pl.semaphore_signal(barrier, inc=1, device_id=device, device_id_type=MESH)

    loads = [
        pltpu.make_async_copy(src, dst, lsem.at[i])
        for i, (src, dst) in enumerate([(w_hbm, w_ref), (x_hbm, x_ref), (wo_hbm, wo_ref)])
    ]
    for load in loads:
        load.start()
    sent = []

    class Transfer:
        def __init__(self, src, dst, device, sends=None, receives=None):
            slot = len(sent)
            self.copy = pltpu.make_async_remote_copy(
                src_ref=src, dst_ref=dst, send_sem=ssem.at[slot], recv_sem=rsem.at[slot],
                device_id=device, device_id_type=MESH,
            )
            self.sends, self.receives = sends, receives
            sent.append(self)
            self.only(sends, self.copy.start)

        def only(self, condition, act):
            if condition is None:
                act()
            else:
                pl.when(condition)(lambda: act())

        def wait_recv(self):
            self.only(self.receives, self.copy.wait_recv)

        def wait_send(self):
            self.only(self.sends, self.copy.wait_send)

    send = Transfer

    def normalize(rows):
        values = rows.astype(F32)
        center = values - jnp.mean(values, axis=-1, keepdims=True)
        spread = jnp.mean(center * center, axis=-1, keepdims=True)
        return (center * lax.rsqrt(spread + EPS) * gin_ref[...]).astype(BF16)

    def project(normed, weights):
        half = jnp.dot(normed, weights, preferred_element_type=F32) * 0.5
        return silu_of_half(half).astype(BF16)

    loads[0].wait()
    ws[...] = w_ref[...].reshape(1024, 1024)
    loads[1].wait()
    loads[2].wait()

    for i in range(4):
        quarter = pl.ds(pl.multiple_of(i * CHUNK + h * 64, 64), 64)
        nq[i * 64 : i * 64 + 64, :] = normalize(x_ref[quarter, :])

    cp[...] = project(normalize(cx_ref[...]), ws[...])
    for head in range(2):
        qall[head, 0, 0, 0, 0:CARDS, :] = cp[:, 512 + head * 128 : 640 + head * 128]
    cut = ccut_ref[...]
    row = lax.broadcasted_iota(jnp.int32, (META, 128), 0)
    told = jnp.where(row == 0, lax.shift_right_logical(cut, 8), cut & 255)
    told = jnp.where(row == 2, csurf_ref[...], told).astype(F32).astype(BF16)
    for head in range(2):
        qall[head, 0, 0, 0, CARDS:, :] = told

    pl.semaphore_wait(barrier, len(greeted))
    near, far = (at_x, at_z), (at_z, at_x)
    q_y = send(qall.at[:, 0, 0, 0], qall.at[:, 0, 0, 1], at_y())
    okay_in = [send(valid_ref, hv.at[b], at_c(b + 1)) for b in (0, 1)]

    def part(quarter_of, i):
        return pl.ds(pl.multiple_of(i * CHUNK + quarter_of * 64, 64), 64)

    def halo_first(i):
        rows = nq.at[pl.ds(i * 64, 64), :]
        return send(rows, hx.at[0, part(h, i), :], at_c(1), c <= 30, c >= 1)

    halo_in = {(0, i): halo_first(i) for i in (3, 2, 1, 0)}
    mine = pl.ds(pl.multiple_of(h * 256, 256), 256)

    lane = lax.broadcasted_iota(jnp.int32, (CARDS, 128), 1).astype(F32)
    surf_t = jnp.transpose(hsurf_ref[...].astype(F32))
    for i in range(8):
        kf[i * 128 : i * 128 + 128, :] = jnp.where(surf_t[:, i : i + 1] == lane, 1.0, 0.0).astype(BF16)

    def only_valid(values, flags, i):
        columns = jnp.transpose(flags.astype(F32))
        okay = jnp.concatenate([columns[:, 2 * i : 2 * i + 1], columns[:, 2 * i + 1 : 2 * i + 2]], 0)
        return (values.astype(F32) * okay).astype(BF16)

    def hist_chunk(i):
        at = slice(i * CHUNK, i * CHUNK + CHUNK)
        proj = project(normalize(x_ref[at, :]), ws[...])
        uh[at, :] = proj[:, 0:256]
        qh[at, :] = proj[:, 512:768]
        kv[at, 0:256] = proj[:, 768:1024]
        kv[at, 256:512] = only_valid(proj[:, 256:512], valid_ref[...], i)

    hist_chunk(0)
    q_y.wait_recv()
    q_near = []
    for head in range(2):
        for d in (1, 3, 2):
            q_near.append(send(qall.at[head, 0, 0], qall.at[head, 0, d], near[head](d)))
    q_far = {(head, d): [] for head in range(2) for d in (1, 2, 3)}
    for head in range(2):
        for d in (1, 3):
            pass
    for i in (1, 2, 3):
        hist_chunk(i)
    halo_y, halo_core = {}, {}

    def halo_pass(b, i):
        halo_in[b, i].wait_recv()
        block = hx.at[b, part(h, i), :]
        known = c >= b + 1
        if b == 0:
            halo_in[1, i] = send(
                block, hx.at[1, part(h, i), :], at_c(1), (c >= 1) & (c <= 30), c >= 2
            )
        halo_y[b, i] = send(block, block, y_peer, known, known)
        halo_core[b, i] = [send(block, block, core_peer, known, known)]

    def halo_pass_on(b, i):
        halo_y[b, i].wait_recv()
        block = hx.at[b, part((h + 2) % 4, i), :]
        known = c >= b + 1
        halo_core[b, i].append(send(block, block, core_peer, known, known))

    def halo_whole(b, i):
        for copy in halo_core[b, i]:
            copy.wait_recv()

    for i in (3, 2, 1, 0):
        halo_pass(0, i)
    for copy in q_near:
        copy.wait_recv()
    for head in range(2):
        for d in (1, 3):
            q_far[head, d].append(
                send(qall.at[head, 0], qall.at[head, d], far[head](d))
            )

    def attend(queries, keys, values, mask):
        half = lax.dot_general(queries, keys, NT, preferred_element_type=F32) * HALF_SCALE
        weights = silu_of_half(half)
        if mask is not None:
            weights = jnp.where(mask(weights.shape), weights, 0.0)
        return jnp.dot(weights.astype(BF16), values, preferred_element_type=F32)

    def hist_tile(keys_ref, j, lo, hi, mask):
        ks = slice(j * CHUNK, j * CHUNK + CHUNK)
        out = []
        for head in range(2):
            a, b = head * 128, head * 128 + 128
            out.append(attend(qh[lo:hi, a:b], keys_ref[ks, a:b], keys_ref[ks, 256 + a : 256 + b], mask))
        return jnp.concatenate(out, 1)

    def not_later(shape):
        return lax.broadcasted_iota(jnp.int32, shape, 1) <= lax.broadcasted_iota(jnp.int32, shape, 0)

    start = (c * 1024).astype(F32)

    def cand_plane(head, d):
        a, b = head * 128, head * 128 + 128
        row = lax.broadcasted_iota(jnp.int32, (8, 128), 0)
        for n in range(4):
            for dy in range(2):
                told = qall[head, d, n, dy, CARDS:, :].astype(F32)
                local = told[0:1, :] * 256.0 + told[1:2, :] - start
                both = jnp.transpose(jnp.where(row == 0, local, told[2:3, :]))
                r = (n * 2 + dy) * 128
                lcb[r : r + 128, :] = jnp.broadcast_to(both[:, 0:1], (128, 128))
                qf[r : r + 128, :] = jnp.where(both[:, 1:2] == lane, 0.0, -FAR).astype(BF16)
        queries = jnp.concatenate(
            [qall[head, d, n, dy, 0:CARDS, :] for n in range(4) for dy in range(2)], 0
        )
        queries = jnp.concatenate([queries, qf[...]], 1)
        total = None
        for j in range(4):
            ks = slice(j * CHUNK, j * CHUNK + CHUNK)
            keys = jnp.concatenate([kv[ks, a:b], kf[ks, :]], 1)

            def mask(shape):
                place = (lax.broadcasted_iota(jnp.int32, shape, 1) + j * CHUNK).astype(F32)
                return place < jnp.concatenate([lcb[...], lcb[...]], 1)

            piece = attend(queries, keys, kv[ks, 256 + a : 256 + b], mask)
            total = piece if total is None else total + piece
        return total

    p_far = []

    def serve(head, d):
        pz[head, d - 1] = cand_plane(head, d).astype(BF16)
        p_far.append(send(pz.at[head, d - 1], rz.at[head, d - 1], far[head](-d)))

    def halo_project(b, i):
        at = slice(i * CHUNK, i * CHUNK + CHUNK)
        weights = jnp.concatenate([ws[:, 768:1024], ws[:, 256:512]], 1)
        proj = project(hx[b, at, :], weights)
        hkv[b, at, 0:256] = proj[:, 0:256]
        hkv[b, at, 256:512] = only_valid(proj[:, 256:512], hv[b], i)

    attn[...] = hist_tile(kv, 0, 0, 1024, not_later)
    for j in (1, 2, 3):
        attn[j * CHUNK :, :] += hist_tile(kv, j, j * CHUNK, 1024, not_later)
    own[0] = cand_plane(0, 0)
    for i in (3, 2):
        halo_pass_on(0, i)
        halo_pass(1, i)
    for i in (1, 0):
        halo_pass_on(0, i)
        halo_pass(1, i)
    for head in range(2):
        for d in (1, 3):
            for copy in q_far[head, d]:
                copy.wait_recv()
    for d, blocks in ((1, pl.ds(0, 2)), (3, pl.ds(2, 2))):
        q_far[0, 2].append(send(qall.at[0, d, blocks], qall.at[0, 2, blocks], at_z(2 - d)))
        q_far[1, 2].append(send(qall.at[1, d, blocks], qall.at[1, 2, blocks], at_x(2 - d)))
    serve(0, 1)
    serve(1, 1)
    serve(0, 3)
    serve(1, 3)
    for head in range(2):
        for copy in q_far[head, 2]:
            copy.wait_recv()
        serve(head, 2)
    for i in (3, 2, 1, 0):
        halo_pass_on(1, i)
    own[1] = cand_plane(1, 0)
    into = []
    for d in (1, 2, 3):
        theirs = pl.ds(pl.multiple_of(((h + d) % 4) * 256, 256), 256)
        into.append(send(wo_ref.at[:, theirs], wc.at[mine, :], at_h(d)))
    wc[mine, :] = wo_ref[:, mine]

    for copy in okay_in:
        copy.wait_recv()
    for i in range(4):
        halo_whole(0, i)
    for i in range(4):
        halo_project(0, i)

    @pl.when(c >= 1)
    def _():
        for j in range(4):
            attn[...] += hist_tile(hkv.at[0], j, 0, 1024, None)

    for copy in p_far:
        copy.wait_recv()
    p_near = []
    for head in range(2):
        total = own[head]
        for d in (1, 2, 3):
            total += rz[head, d - 1].astype(F32)
        px[head] = total.astype(BF16)
        own[head, 0:256, :] = total[0:256]
        for d in (1, 3, 2):
            p_near.append(
                send(px.at[head, pl.ds(d * 256, 256)], rx.at[head, d - 1], near[head](-d))
            )

    full = 1024.0

    def chunk_rows(i):
        return (slice(i * CHUNK, i * CHUNK + CHUNK), CHUNK) if i < 4 else (slice(1024, 1152), CARDS)

    def stats_out(i, values):
        size = values.shape[0]
        sums = jnp.sum(values, axis=-1, keepdims=True)
        squares = jnp.sum(values * values, axis=-1, keepdims=True)
        spread = lax.broadcasted_iota(jnp.int32, (size, 128), 1)
        st[0, i, :, 0:size] = jnp.transpose(jnp.where(spread == 0, sums, squares))[0:8, :]
        return [send(st.at[0, i], st.at[d, i], at_h(d)) for d in (1, 2, 3)]

    def gate_out(i, values, update, got):
        at, size = chunk_rows(i)
        for copy in got:
            copy.wait_recv()
        both = (st[0, i] + st[1, i] + st[2, i] + st[3, i])[:, 0:size] / full
        both = jnp.transpose(both)
        mean, square = both[:, 0:1], both[:, 1:2]
        gated = (values - mean) * lax.rsqrt(square - mean * mean + EPS) * gout_ref[...] * update.astype(F32)
        gf[at, mine] = gated.astype(BF16)
        block = gf.at[at, mine]
        return [
            send(block, block, core_peer),
            send(block, block, y_peer),
        ]

    across = pl.ds(pl.multiple_of(((h + 2) % 4) * 256, 256), 256)

    def gate_forward(i, moving):
        at, _ = chunk_rows(i)
        moving[1].wait_recv()
        block = gf.at[at, across]
        moving.append(send(block, block, core_peer))

    def finish(i, moving, rows_ref, out_ref):
        at, size = chunk_rows(i)
        moving[0].wait_recv()
        moving[2].wait_recv()
        where = at if i < 4 else slice(0, CARDS)
        mixed = jnp.dot(gf[at, :], wc[...], preferred_element_type=F32)
        out_ref[where, :] = (rows_ref[where, mine].astype(F32) + mixed).astype(BF16)

    got, moving = {}, {}
    for i in (3, 2, 1, 0):
        halo_whole(1, i)
        halo_project(1, i)

        @pl.when(c >= 2)
        def _():
            def later(shape):
                return (
                    lax.broadcasted_iota(jnp.int32, shape, 1) + i * CHUNK
                    > lax.broadcasted_iota(jnp.int32, shape, 0)
                )

            hi = i * CHUNK + CHUNK
            attn[0:hi, :] += hist_tile(hkv.at[1], i, 0, hi, later)

        got[i] = stats_out(i, attn[chunk_rows(i)[0], :])

    def gate_hist(i):
        where = chunk_rows(i)[0]
        moving[i] = gate_out(i, attn[where, :], uh[where, :], got[i])

    for copy in p_near:
        copy.wait_recv()
    for head in range(2):
        total = own[head, 0:256, :]
        for d in (1, 2, 3):
            total += rx[head, d - 1].astype(F32)
        own[head, 0:CARDS, :] = total[0:CARDS]
        py[head] = total[CARDS:]
    p_y = send(py, ry, at_y())
    gate_hist(3)
    gate_hist(2)
    selfs = []
    for head in range(2):
        a, b = head * 128, head * 128 + 128
        query = cp[:, 512 + a : 512 + b].astype(F32)
        key = cp[:, 768 + a : 768 + b].astype(F32)
        half = jnp.sum(query * key, axis=-1, keepdims=True) * HALF_SCALE
        weight = silu_of_half(half).astype(BF16).astype(F32)
        selfs.append(weight * cp[:, 256 + a : 256 + b].astype(F32))
    p_y.wait_recv()
    for head in range(2):
        a, b = head * 128, head * 128 + 128
        cattn[:, a:b] = own[head, 0:CARDS, :] + ry[head] + selfs[head]
    got[4] = stats_out(4, cattn[...])
    gate_hist(1)
    gate_hist(0)
    moving[4] = gate_out(4, cattn[...], cp[:, 0:256], got[4])
    gate_forward(3, moving[3])
    for copy in into:
        copy.wait_recv()
    gate_forward(2, moving[2])
    finish(3, moving[3], x_ref, oh_ref)
    gate_forward(1, moving[1])
    finish(2, moving[2], x_ref, oh_ref)
    gate_forward(0, moving[0])
    finish(1, moving[1], x_ref, oh_ref)
    gate_forward(4, moving[4])
    finish(0, moving[0], x_ref, oh_ref)
    finish(4, moving[4], cx_ref, oc_ref)
    for copy in sent:
        copy.wait_send()


def shards(
    history,
    candidates,
    history_valid,
    history_surface,
    candidate_surface,
    candidate_cutoff,
    gain_in,
    w_uvqk,
    gain_out,
    w_out,
):
    vmem = pl.BlockSpec(memory_space=pltpu.VMEM)
    hbm = pl.BlockSpec(memory_space=pl.ANY)
    return pl.pallas_call(
        kernel,
        out_shape=(
            jax.ShapeDtypeStruct((1024, 256), BF16),
            jax.ShapeDtypeStruct((CARDS, 256), BF16),
        ),
        in_specs=[hbm] + [vmem] * 6 + [hbm, vmem, hbm],
        out_specs=(vmem, vmem),
        scratch_shapes=[
            pltpu.VMEM((1024, 1024), BF16),
            pltpu.VMEM((1024, 4, 256), BF16),
            pltpu.VMEM((256, 1024), BF16),
            pltpu.VMEM((1024, 1024), BF16),
            pltpu.VMEM((256, 1024), BF16),
            pltpu.VMEM((2, 1024, 1024), BF16),
            pltpu.VMEM((2, 8, 128), jnp.int32),
            pltpu.VMEM((1024, 512), BF16),
            pltpu.VMEM((2, 1024, 512), BF16),
            pltpu.VMEM((1024, 256), BF16),
            pltpu.VMEM((1024, 256), BF16),
            pltpu.VMEM((CARDS, 1024), BF16),
            pltpu.VMEM((1024, 128), BF16),
            pltpu.VMEM((2, 4, 4, 2, CARDS + META, 128), BF16),
            pltpu.VMEM((1024, 128), BF16),
            pltpu.VMEM((1024, 128), F32),
            pltpu.VMEM((2, 1024, 128), F32),
            pltpu.VMEM((2, 3, 1024, 128), BF16),
            pltpu.VMEM((2, 3, 1024, 128), BF16),
            pltpu.VMEM((2, 1024, 128), BF16),
            pltpu.VMEM((2, 3, 256, 128), BF16),
            pltpu.VMEM((2, CARDS, 128), F32),
            pltpu.VMEM((2, CARDS, 128), F32),
            pltpu.VMEM((1024, 256), F32),
            pltpu.VMEM((CARDS, 256), F32),
            pltpu.VMEM((4, 5, 8, 256), F32),
            pltpu.VMEM((1152, 1024), BF16),
            pltpu.VMEM((1024, 256), BF16),
            pltpu.SemaphoreType.DMA((N_SEM,)),
            pltpu.SemaphoreType.DMA((N_SEM,)),
            pltpu.SemaphoreType.DMA((3,)),
        ],
        compiler_params=pltpu.CompilerParams(
            collective_id=0, has_side_effects=True, vmem_limit_bytes=56 * 2**20
        ),
        name="hstu",
    )(
        history,
        candidates,
        history_valid.reshape(8, 128),
        history_surface.reshape(8, 128),
        candidate_surface.reshape(1, CARDS),
        candidate_cutoff.reshape(1, CARDS),
        gain_in.reshape(1, 1024),
        w_uvqk,
        gain_out.reshape(1, 256),
        w_out,
    )


def solution(mesh):
    placed = (
        P("ctx", None),
        P("ctx", None),
        P("ctx"),
        P("ctx"),
        P("ctx"),
        P("ctx"),
        P(),
        P(None, None, "cand"),
        P("cand"),
        P("cand", None),
    )
    return jax.shard_map(
        shards,
        mesh=mesh,
        in_specs=placed,
        out_specs=(P("ctx", "cand"), P("ctx", "cand")),
        check_vma=False,
    )
```
